256 devices in a mesh: member: 8 (over y, z_hi), grid: 32 (over x, z_lo, core).
Axes of the slice: x: 4, y: 4, z: 8 (z_hi: 2, z_lo: 4; z = z_hi * 4 + z_lo), core: 2. Of those that a mesh axis runs over, the one named last changes fastest.
Arguments:
- hidden: bfloat16 [8, 65536, 1024], P('member', 'grid'), may hold values from -6 to 6
- pred: bfloat16 [8, 100, 65536], P('member', None, 'grid'), may hold values from -6 to 6
- target: bfloat16 [100, 65536], P(None, 'grid'), may hold values from -6 to 6
- area: float32 [65536], P('grid'), may hold values from 0.5 to 5
- var_weight: float32 [100], replicated, may hold values from 0.5 to 5
- w_in: bfloat16 [1024, 1024], replicated, may hold values from -0.1875 to 0.1875
- w_out: bfloat16 [1024, 100], replicated, may hold values from -0.1875 to 0.1875
Outputs:
- hidden_grad: bfloat16 [8, 65536, 1024], P('member', 'grid')
- w_in_grad: float32 [1024, 1024], P('grid')
- w_out_grad: float32 [1024, 100], P('grid')
The draws below stay inside these ranges and needn't reach their ends.
All inputs are finite; a program needn't handle non-finite values.
Results may differ from the reference program's by a relative error of at most 0.0061.
Values may be sent and summed in bfloat16 or wider, within the bound.
A program may use at most 128 MiB of HBM per device.

```python
import math
import jax
import jax.numpy as jnp
from jax import lax

H = 1024
V = 100
MEMBERS = 8
NPTS = 65536
TOTAL_ROWS = 524288


def raised(entries, rng, source, target, shards_of, factor):
    owner, partner = [(jnp.arange(entries.shape[dim]) // (entries.shape[dim] // shards_of)).reshape([-1 if axis == dim else 1 for axis in range(entries.ndim)]) for dim in (source, target)]
    chosen = jax.random.permutation(rng, shards_of)[partner]
    strong = (owner == chosen) | (owner == (partner + shards_of // 2) % shards_of)
    return jnp.where(strong, factor * entries, entries)


def block_scale(stream_key, shape, cuts, least, high):
    gain, own = 1.0, jax.random.fold_in(stream_key, 6)
    for axis_at, blocks in cuts:
        steps = jnp.exp(jax.random.uniform(jax.random.fold_in(own, axis_at), (blocks,), jnp.float32, least / len(cuts), high / len(cuts)))
        gain = gain * jnp.repeat(steps, shape[axis_at] // blocks).reshape([-1 if axis == axis_at else 1 for axis in range(len(shape))])
    return gain


def centred(stream_key, shape, deviation, reach, shards=(), held_as=jnp.bfloat16):
    entries = jax.random.normal(stream_key, shape, jnp.float32) * deviation
    if len(shards) > 0:
        entries = block_scale(stream_key, shape, shards, -0.22, 0.18) * entries
    return jnp.clip(entries, min=-reach, max=reach).astype(held_as)


def noise_with(own_key, extent, scale, bound, split, heavy, held_as=jnp.bfloat16):
    array = scale * jax.random.normal(own_key, extent, jnp.float32)
    if split:
        array = array * block_scale(own_key, extent, split, -0.22, 0.18)
    return jnp.clip(raised(array, jax.random.fold_in(own_key, 3), *heavy), -bound, bound).astype(held_as)


def setup_inputs(seed: int = 0) -> dict:
    arg_keys = jax.random.split(jax.random.key(seed), 8)
    return {
        "hidden": noise_with(arg_keys[0], (MEMBERS, NPTS, H), 1.0, 6.0, ((0, 8), (1, 32)), (1, 2, 32, 2.75)),
        "pred": centred(arg_keys[1], (MEMBERS, V, NPTS), 1.0, 6.0, ((0, 8), (2, 32))),
        "target": centred(arg_keys[2], (V, NPTS), 1.0, 6.0, ((1, 32),)),
        "area": jnp.clip(jnp.exp(math.log(5.0) - 2.3025851 * jax.random.uniform(arg_keys[3], (NPTS,), jnp.float32) ** block_scale(arg_keys[3], (NPTS,), ((0, 32),), -0.2, 0.2)), 0.5, 5.0),
        "var_weight": jnp.clip(jnp.exp(jax.random.uniform(arg_keys[4], (V,), jnp.float32, math.log(0.5), math.log(5.0))), 0.5, 5.0),
        "w_in": centred(arg_keys[5], (H, H), H ** -0.5, 0.1875),
        "w_out": centred(arg_keys[6], (H, V), H ** -0.5, 0.1875),
    }


def reference(hidden, pred, target, area, var_weight, w_in, w_out):
    members = MEMBERS
    weight = var_weight[:, None] * area[None, :]
    preds = pred.astype(jnp.float32)
    spread = jnp.zeros(preds.shape, jnp.float32)
    for other in range(members):
        term = (weight[None] * jnp.sign(preds - preds[other][None])).astype(jnp.bfloat16)
        term = lax.optimization_barrier(term)
        spread = spread + term.astype(jnp.float32)
    grad = weight[None] * jnp.sign(preds - target.astype(jnp.float32)[None]) / members
    grad = (grad - spread / (members * (members - 1))).astype(jnp.bfloat16)

    def member_step(carry, inputs):
        acc_in, acc_out = carry
        rows, grad_m = inputs
        pre = jnp.dot(rows, w_in, preferred_element_type=jnp.float32)
        act = jax.nn.gelu(pre).astype(jnp.bfloat16)
        act_grad = jnp.dot(grad_m.T, w_out.T, preferred_element_type=jnp.float32)
        pre_grad = jax.vjp(jax.nn.gelu, pre)[1](act_grad)[0].astype(jnp.bfloat16)
        rows_grad = jnp.dot(pre_grad, w_in.T, preferred_element_type=jnp.float32).astype(jnp.bfloat16)
        acc_in = acc_in + jnp.dot(rows.T, pre_grad, preferred_element_type=jnp.float32)
        acc_out = acc_out + jnp.dot(act.T, grad_m.T, preferred_element_type=jnp.float32)
        return ((acc_in, acc_out), rows_grad)
    start = (jnp.zeros((H, H), jnp.float32), jnp.zeros((H, V), jnp.float32))
    (acc_in, acc_out), hidden_grad = lax.scan(member_step, start, (hidden, grad))
    scale = 1.0 / math.sqrt(TOTAL_ROWS)
    return (hidden_grad, acc_in * scale, acc_out * scale)
```

```python
import functools
import math

import jax
import jax.numpy as jnp
from jax import lax
from jax.experimental import pallas as pl
from jax.experimental.pallas import tpu as pltpu
from jax.sharding import PartitionSpec as P

BF = jnp.bfloat16
F32 = jnp.float32
MEMBERS = 8
V = 100
VS = 112
VP = 128
NCH = 2
BLK = 256
WB = 512
NWB = 2
ROOT = math.sqrt(2.0 / math.pi)


def dot(a, b):
    return jnp.dot(a, b, preferred_element_type=F32)


def dot_nt(a, b):
    return lax.dot_general(a, b, (((1,), (1,)), ((), ())), preferred_element_type=F32)


def kernel(
    scale,
    hid_hbm, pred_hbm, tgt_hbm, area, vw, win_hbm, wout,
    hg_hbm, win_out, wout_out,
    hid, win, hT, act, gp, pg, hgs, wop, woT,
    prcv, tgt, gout, gbuf,
    csnd, crcv, own, cosnd, corcv, oown,
    s1, s1o, r1a, r1b, r1o, a2, b2,
    s2a, s2b, r2a, r2b, s3, r3, s4, r4,
    lsem, hsem, osem, psem, gsem, csem, x1sem, y1sem, o1sem, a2sem, b2sem, z3sem, y4sem,
):
    points = hid.shape[0]
    width = hid.shape[1]
    half = points // NCH
    m = lax.axis_index("member")
    g = lax.axis_index("grid")
    y, z_hi = m // 2, m % 2
    x, z_lo, core = g // 8, (g // 2) % 4, g % 2
    z = z_hi * 4 + z_lo

    def dev(xx, yy, zz, cc):
        return (yy * 2 + zz // 4, (xx * 4 + zz % 4) * 2 + cc)

    def member_dev(mm):
        return (mm, g)

    def remote(src, dst, sems, j, target):
        return pltpu.make_async_remote_copy(
            src_ref=src, dst_ref=dst, send_sem=sems.at[0, j], recv_sem=sems.at[1, j],
            device_id=target, device_id_type=pl.DeviceIdType.MESH,
        )

    barrier = pltpu.get_barrier_semaphore()
    partners = [member_dev((m + j) % MEMBERS) for j in range(1, MEMBERS)]
    partners += [dev(x, y, (z + j) % 8, core) for j in (1, 2, 3, 5, 6, 7)]
    partners += [dev((x + j) % 4, y, z, core) for j in (1, 2, 3)]
    partners += [dev(x, y, z, 1 - core)]
    for partner in partners:
        pl.semaphore_signal(barrier, inc=1, device_id=partner, device_id_type=pl.DeviceIdType.MESH)

    win_copy = pltpu.make_async_copy(win_hbm, win, lsem.at[0])
    win_copy.start()

    def hid_copy(i):
        rows = pl.ds(pl.multiple_of(i * BLK, BLK), BLK)
        return pltpu.make_async_copy(hid_hbm.at[0, rows], hid.at[rows], hsem.at[i])

    hid_copy(0).start()
    own_copies = []
    for c in range(NCH):
        cols = pl.ds(pl.multiple_of(c * half + 128 * m, 128), 128)
        own_copies.append(pltpu.make_async_copy(pred_hbm.at[0, :, cols], prcv.at[c, m], lsem.at[1 + 2 * c]))
        own_copies.append(pltpu.make_async_copy(tgt_hbm.at[:, cols], tgt.at[c], lsem.at[2 + 2 * c]))
    for copy in own_copies:
        copy.start()
    for i in range(1, points // BLK):
        hid_copy(i).start()

    gbuf[...] = jnp.zeros_like(gbuf)
    gout[...] = jnp.zeros_like(gout)
    wop[...] = jnp.zeros_like(wop)
    wop[:, :V] = wout[...]
    woT[...] = jnp.transpose(wop[...])
    rows_at = lax.broadcasted_iota(jnp.int32, (V, V), 0)
    cols_at = lax.broadcasted_iota(jnp.int32, (V, V), 1)
    vcol = jnp.sum(jnp.where(rows_at == cols_at, jnp.broadcast_to(vw[...], (V, V)), 0.0), axis=1, keepdims=True)
    win_copy.wait()

    def forward(i, carry):
        hid_copy(i).wait()
        rows = pl.ds(pl.multiple_of(i * BLK, BLK), BLK)
        h = hid[rows, :]
        for n in range(0, width, 256):
            u = dot(h, win[:, n:n + 256])
            square = u * u
            t = jnp.tanh(u * (square * (ROOT * 0.044715) + ROOT))
            p = 0.5 * t + 0.5
            a = u * p
            act[rows, n:n + 256] = a.astype(BF)
            gp[rows, n:n + 256] = p + (a * (1.0 - p)) * (square * (ROOT * 0.044715 * 6.0) + 2.0 * ROOT)
        for t8 in range(width // 128):
            turned = jnp.transpose(h[:, t8 * 128:t8 * 128 + 128])
            for q in range(4):
                zl, cc = (t8 % 2) * 2 + q // 2, q % 2
                first = (t8 // 2) * 128 + zl * 32
                hT[cc, first:first + 32, rows] = turned[q * 32:q * 32 + 32, :]
        return carry

    steps = points // BLK
    before = steps // 2
    lax.fori_loop(0, before, forward, 0)

    pl.semaphore_wait(barrier, len(partners))
    pred_copies = []
    for c in range(NCH):
        chunk = []
        for j in range(1, MEMBERS):
            to = (m + j) % MEMBERS
            cols = pl.ds(pl.multiple_of(c * half + 128 * to, 128), 128)
            copy = remote(pred_hbm.at[0, :, cols], prcv.at[c, m], psem.at[c], j, member_dev(to))
            copy.start()
            chunk.append(copy)
        pred_copies.append(chunk)

    lax.fori_loop(before, steps, forward, 0)

    grad_copies = []
    for c in range(NCH):
        own_copies[2 * c].wait()
        own_copies[2 * c + 1].wait()
        for copy in pred_copies[c]:
            copy.wait_recv()
        cols = pl.ds(pl.multiple_of(c * half + 128 * m, 128), 128)
        weight = vcol * area[:, cols]
        rounded = weight.astype(BF).astype(F32)
        aim = tgt[c].astype(F32)
        preds = [prcv[c, k].astype(F32) for k in range(MEMBERS)]
        counts = [None] * MEMBERS
        for i in range(MEMBERS):
            for k in range(i):
                s = jnp.where(preds[i] > preds[k], 1.0, jnp.where(preds[i] < preds[k], -1.0, 0.0))
                counts[i] = s if counts[i] is None else counts[i] + s
                counts[k] = -s if counts[k] is None else counts[k] - s
        for k in range(MEMBERS):
            s = jnp.where(preds[k] > aim, 1.0, jnp.where(preds[k] < aim, -1.0, 0.0))
            grad = weight * s / MEMBERS - (rounded * counts[k]) / (MEMBERS * (MEMBERS - 1))
            gout[c, k, :V, :] = grad.astype(BF)
        chunk = []
        for j in range(1, MEMBERS):
            to = (m + j) % MEMBERS
            copy = remote(gout.at[c, to], gbuf.at[pl.ds(0, VS), cols], gsem.at[c], j, member_dev(to))
            copy.start()
            chunk.append(copy)
        gbuf[0:VS, cols] = gout[c, m]
        grad_copies.append(chunk)

    def back(i, carry):
        rows = pl.ds(pl.multiple_of(i * 128, 128), 128)
        turned = jnp.transpose(gbuf[:, rows])
        for n in range(0, width, 512):
            pg[rows, n:n + 512] = (dot(turned, woT[:, n:n + 512]) * gp[rows, n:n + 512]).astype(BF)
        return carry

    def hg_copy(i):
        rows = pl.ds(pl.multiple_of(i * BLK, BLK), BLK)
        return pltpu.make_async_copy(hgs.at[rows], hg_hbm.at[0, rows], osem.at[i])

    def hidden_step(i, carry):
        rows = pl.ds(pl.multiple_of(i * BLK, BLK), BLK)
        for n in range(0, width, 256):
            hgs[rows, n:n + 256] = dot_nt(pg[rows, :], win[n:n + 256, :]).astype(BF)
        hg_copy(i).start()
        return carry

    per = half // BLK
    for c in range(NCH):
        for copy in grad_copies[c]:
            copy.wait_recv()
        lax.fori_loop(c * (half // 128), (c + 1) * (half // 128), back, 0)
        if c < NCH - 1:
            lax.fori_loop(c * per, (c + 1) * per, hidden_step, 0)

    other = 1 - core
    sibling = dev(x, y, z, other)


    def rows4(value, parts):
        return value.reshape((parts, value.shape[0] // parts) + value.shape[1:])

    core_copies = []
    x1, y1 = [], []
    for b in range(NWB):
        for mm in range(2):
            for n in range(0, WB, 256):
                csnd[b, mm * 256:mm * 256 + 256, n:n + 256] = dot(
                    hT[other, mm * 256:mm * 256 + 256, :], pg[:, b * WB + n:b * WB + n + 256]
                ).astype(BF)
        copy = remote(csnd.at[b], crcv.at[b], csem, b, sibling)
        copy.start()
        core_copies.append(copy)
        for mm in range(2):
            for n in range(0, WB, 256):
                own[b, 2 * mm:2 * mm + 2, :, n:n + 256] = rows4(
                    dot(hT[core, mm * 256:mm * 256 + 256, :], pg[:, b * WB + n:b * WB + n + 256]), 2
                )
        copy.wait_recv()
        for q in range(4):
            total = own[b, q] + crcv[b, q * 128:q * 128 + 128, :].astype(F32)
            own[b, q] = total
            s1[b, q] = total.astype(BF)
        for j in (1, 2, 3):
            xx, yy = (x + j) % 4, (y + j) % 4
            copy = remote(s1.at[b, xx, pl.ds(0, 64)], r1a.at[b, x], x1sem.at[b], j, dev(xx, y, z, core))
            copy.start()
            x1.append(copy)
            cols = pl.ds(pl.multiple_of(yy * 128, 128), 128)
            copy = remote(s1.at[b, :, pl.ds(64, 64), cols], r1b.at[b, y], y1sem.at[b], j, dev(x, yy, z, core))
            copy.start()
            y1.append(copy)
        if b == 0:
            for h8 in range(width // 128):
                turned = jnp.transpose(dot(gbuf[...], act[:, h8 * 128:h8 * 128 + 128]))
                for q in range(4):
                    zl, cc = (h8 % 2) * 2 + q // 2, q % 2
                    first = (h8 // 2) * 128 + zl * 32
                    oown[cc, first:first + 32, :] = turned[q * 32:q * 32 + 32, :]
            cosnd[...] = oown[other].astype(BF)
            ocopy = remote(cosnd, corcv, csem, NWB, sibling)
            ocopy.start()
            core_copies.append(ocopy)
    ocopy.wait_recv()
    total = oown[core] + corcv[...].astype(F32)
    oown[core] = total
    s1o[...] = rows4(total.astype(BF), 4)
    o1 = []
    for j in (1, 2, 3):
        xx = (x + j) % 4
        copy = remote(s1o.at[xx], r1o.at[x], o1sem, j, dev(xx, y, z, core))
        copy.start()
        o1.append(copy)

    lax.fori_loop((NCH - 1) * per, NCH * per, hidden_step, 0)

    own_cols = pl.ds(pl.multiple_of(y * 128, 128), 128)
    for copy in x1 + y1 + o1:
        copy.wait_recv()
    for b in range(NWB):
        ta = own[b, x, 0:64, :]
        tb = own[b, :, 64:128, own_cols]
        for j in (1, 2, 3):
            ta = ta + r1a[b, (x + j) % 4].astype(F32)
            tb = tb + r1b[b, (y + j) % 4].astype(F32)
        a2[b] = ta
        b2[b] = tb
        for q in range(4):
            s2a[q, 64 * b:64 * b + 64, :] = ta[:, q * 128:q * 128 + 128].astype(BF)
            s2b[q, 64 * b:64 * b + 64, :] = tb[q].astype(BF)
    to = oown[core, pl.ds(pl.multiple_of(x * 128, 128), 128), :]
    for j in (1, 2, 3):
        to = to + r1o[(x + j) % 4].astype(F32)
    oown[core, pl.ds(pl.multiple_of(x * 128, 128), 128), :] = to
    for q in range(4):
        s2a[q, 128:160, :] = to[q * 32:q * 32 + 32, :].astype(BF)
    second = []
    for j in (1, 2, 3):
        xx, yy = (x + j) % 4, (y + j) % 4
        copy = remote(s2a.at[yy], r2a.at[y], a2sem, j, dev(x, yy, z, core))
        copy.start()
        second.append(copy)
        copy = remote(s2b.at[xx], r2b.at[x], b2sem, j, dev(xx, y, z, core))
        copy.start()
        second.append(copy)
    for copy in second:
        copy.wait_recv()

    for b in range(NWB):
        ta = a2[b, :, own_cols]
        tb = b2[b, x]
        for j in (1, 2, 3):
            ta = ta + r2a[(y + j) % 4, 64 * b:64 * b + 64, :].astype(F32)
            tb = tb + r2b[(x + j) % 4, 64 * b:64 * b + 64, :].astype(F32)
        s4[0:64, :] = ta
        s4[64:128, :] = tb
        for q in range(4):
            r4[q, 32 * b:32 * b + 32, :] = s4[q * 32:q * 32 + 32, :]
            s3[q, 32 * b:32 * b + 32, :] = s4[q * 32:q * 32 + 32, :].astype(BF)
    to = oown[core, pl.ds(pl.multiple_of(x * 128 + y * 32, 32), 32), :]
    for j in (1, 2, 3):
        to = to + r2a[(y + j) % 4, 128:160, :].astype(F32)
    for q in range(4):
        s3[q, 64:96, :] = to.astype(BF)
    third = []
    for j in range(1, 8):
        zz = (z + j) % 8
        copy = remote(s3.at[zz % 4], r3.at[z], z3sem, j, dev(x, y, zz, core))
        copy.start()
        third.append(copy)
    mine = r4[z_lo, 0:64, :]
    total = jnp.concatenate([mine, to], axis=0)
    for copy in third:
        copy.wait_recv()
    for j in range(1, 8):
        total = total + r3[(z + j) % 8].astype(F32)
    total = total * scale
    s4[0:96, :] = total

    fourth = []
    for j in (1, 2, 3):
        yy = (y + j) % 4
        copy = remote(s4.at[pl.ds(0, 96)], r5(r4).at[y], y4sem, j, dev(x, yy, z, core))
        copy.start()
        fourth.append(copy)
    r4[4 + y] = total
    for copy in fourth:
        copy.wait_recv()
    for q in range(4):
        for b in range(NWB):
            win_out[:, b * WB + q * 128:b * WB + q * 128 + 128] = r4[4 + q, 32 * b:32 * b + 32, :]
    wout_out[...] = r4[4 + z_lo, 64:96, 0:V]

    for chunk in pred_copies + grad_copies:
        for copy in chunk:
            copy.wait_send()
    for copy in core_copies + x1 + y1 + o1 + second + third + fourth:
        copy.wait_send()

    def drain(i, carry):
        hg_copy(i).wait()
        return carry

    lax.fori_loop(0, steps, drain, 0)


def r5(ref):
    return ref.at[pl.ds(4, 4)]


def shards(hidden, pred, target, area, var_weight, w_in, w_out):
    points, width = hidden.shape[1:]
    scale = 1.0 / math.sqrt(points * lax.axis_size("grid") * MEMBERS)
    share = width // lax.axis_size("grid")
    any_spec = pl.BlockSpec(memory_space=pl.ANY)
    vmem_spec = pl.BlockSpec(memory_space=pltpu.VMEM)

    def vm(*shape, dtype=BF):
        return pltpu.VMEM(shape, dtype)

    def sems(*shape):
        return pltpu.SemaphoreType.DMA(shape)

    return pl.pallas_call(
        functools.partial(kernel, scale),
        out_shape=(
            jax.ShapeDtypeStruct(hidden.shape, BF),
            jax.ShapeDtypeStruct((share, width), F32),
            jax.ShapeDtypeStruct((share, V), F32),
        ),
        in_specs=[any_spec, any_spec, any_spec, vmem_spec, vmem_spec, any_spec, vmem_spec],
        out_specs=(any_spec, vmem_spec, vmem_spec),
        scratch_shapes=[
            vm(points, width), vm(width, width), vm(2, width // 2, points), vm(points, width),
            vm(points, width, dtype=F32), vm(points, width), vm(points, width), vm(width, VP), vm(VP, width),
            vm(NCH, MEMBERS, V, 128), vm(NCH, V, 128), vm(NCH, MEMBERS, VS, 128), vm(VP, points),
            vm(NWB, width // 2, WB), vm(NWB, width // 2, WB), vm(NWB, 4, 128, WB, dtype=F32),
            vm(width // 2, VP), vm(width // 2, VP), vm(2, width // 2, VP, dtype=F32),
            vm(NWB, 4, 128, WB), vm(4, 128, VP), vm(NWB, 4, 64, WB), vm(NWB, 4, 4, 64, 128), vm(4, 128, VP),
            vm(NWB, 64, WB, dtype=F32), vm(NWB, 4, 64, 128, dtype=F32),
            vm(4, 160, 128), vm(4, 128, 128), vm(4, 160, 128), vm(4, 128, 128),
            vm(4, 96, 128), vm(8, 96, 128), vm(128, 128, dtype=F32), vm(8, 96, 128, dtype=F32),
            sems(1 + 2 * NCH), sems(points // BLK), sems(points // BLK),
            sems(NCH, 2, MEMBERS), sems(NCH, 2, MEMBERS), sems(2, NWB + 1),
            sems(NWB, 2, 4), sems(NWB, 2, 4), sems(2, 4), sems(2, 4), sems(2, 4), sems(2, 8), sems(2, 4),
        ],
        compiler_params=pltpu.CompilerParams(
            collective_id=0, has_side_effects=True, vmem_limit_bytes=60 * 1024 * 1024
        ),
    )(hidden, pred, target, area.reshape(1, -1), var_weight.reshape(1, -1), w_in, w_out)


def solution(mesh):
    return jax.shard_map(
        shards,
        mesh=mesh,
        in_specs=(
            P("member", "grid", None),
            P("member", None, "grid"),
            P(None, "grid"),
            P("grid"),
            P(),
            P(),
            P(),
        ),
        out_specs=(P("member", "grid", None), P("grid", None), P("grid", None)),
        check_vma=False,
    )
```

```python
import functools
import math

import jax
import jax.numpy as jnp
from jax import lax
from jax.experimental import pallas as pl
from jax.experimental.pallas import tpu as pltpu
from jax.sharding import PartitionSpec as P

BF = jnp.bfloat16
F32 = jnp.float32
MEMBERS = 8
V = 100
VS = 112
VP = 128
NCH = 2
BLK = 256
WB = 512
NWB = 2
ROOT = math.sqrt(2.0 / math.pi)


def dot(a, b):
    return jnp.dot(a, b, preferred_element_type=F32)


def dot_nt(a, b):
    return lax.dot_general(a, b, (((1,), (1,)), ((), ())), preferred_element_type=F32)


def kernel(
    scale,
    hid_hbm, pred_hbm, tgt_hbm, area, vw, win_hbm, wout_t,
    hgs, win_out, wout_out,
    hid, win, hT, act, gp, pg, woT,
    psrc, prcv, tgt, gout, gbuf,
    acc, csnd, crcv, oacc, cosnd, corcv, oown,
    s1, s1o, r1a, r1b, r1o, a2, b2,
    s2a, s2b, r2a, r2b, z4, s3, r3, s4, r4,
    lsem, hsem, psem, gsem, csem, x1sem, y1sem, o1sem, a2sem, b2sem, z3sem, y4sem,
):
    points = hid.shape[0]
    width = hid.shape[1]
    half = points // NCH
    m = lax.axis_index("member")
    g = lax.axis_index("grid")
    y, z_hi = m // 2, m % 2
    x, z_lo, core = g // 8, (g // 2) % 4, g % 2
    z = z_hi * 4 + z_lo

    def dev(xx, yy, zz, cc):
        return (yy * 2 + zz // 4, (xx * 4 + zz % 4) * 2 + cc)

    def member_dev(mm):
        return (mm, g)

    def remote(src, dst, sems, j, target):
        return pltpu.make_async_remote_copy(
            src_ref=src, dst_ref=dst, send_sem=sems.at[0, j], recv_sem=sems.at[1, j],
            device_id=target, device_id_type=pl.DeviceIdType.MESH,
        )

    barrier = pltpu.get_barrier_semaphore()
    partners = [member_dev((m + j) % MEMBERS) for j in range(1, MEMBERS)]
    partners += [dev(x, y, (z + j) % 8, core) for j in (1, 2, 3, 5, 6, 7)]
    partners += [dev((x + j) % 4, y, z, core) for j in (1, 2, 3)]
    partners += [dev(x, y, z, 1 - core)]
    for partner in partners:
        pl.semaphore_signal(barrier, inc=1, device_id=partner, device_id_type=pl.DeviceIdType.MESH)

    win_copy = pltpu.make_async_copy(win_hbm, win, lsem.at[0, 0])
    win_copy.start()

    def hid_copy(i):
        rows = pl.ds(pl.multiple_of(i * BLK, BLK), BLK)
        return pltpu.make_async_copy(hid_hbm.at[0, rows], hid.at[rows], hsem.at[i])

    own_copies, source_copies = [], []
    for c in range(NCH):
        mine = pl.ds(pl.multiple_of(c * half + 128 * m, 128), 128)
        own_copies.append(pltpu.make_async_copy(pred_hbm.at[0, :, mine], prcv.at[c, m], lsem.at[1, c]))
        own_copies.append(pltpu.make_async_copy(tgt_hbm.at[:, mine], tgt.at[c], lsem.at[2, c]))
        for k in range(MEMBERS):
            cols = pl.ds(c * half + 128 * k, 128)
            source_copies.append(pltpu.make_async_copy(pred_hbm.at[0, :, cols], psrc.at[c, k], lsem.at[3 + k, c]))
    for copy in source_copies + own_copies:
        copy.start()
    hid_copy(0).start()
    for i in range(1, points // BLK):
        hid_copy(i).start()


    def forward(i, carry):
        hid_copy(i).wait()
        rows = pl.ds(pl.multiple_of(i * BLK, BLK), BLK)
        h = hid[rows, :]
        for n in range(0, width, 256):
            u = dot(h, win[:, n:n + 256])
            square = u * u
            t = jnp.tanh(u * (square * (ROOT * 0.044715) + ROOT))
            p = 0.5 * t + 0.5
            a = u * p
            act[rows, n:n + 256] = a.astype(BF)
            gp[rows, n:n + 256] = p + (a * (1.0 - p)) * (square * (ROOT * 0.044715 * 6.0) + 2.0 * ROOT)
        for t8 in range(width // 128):
            turned = jnp.transpose(h[:, t8 * 128:t8 * 128 + 128])
            for q in range(4):
                zl, cc = (t8 % 2) * 2 + q // 2, q % 2
                first = (t8 // 2) * 128 + zl * 32
                hT[cc, first:first + 32, rows] = turned[q * 32:q * 32 + 32, :]
        return carry

    steps = points // BLK

    for copy in source_copies:
        copy.wait()
    pl.semaphore_wait(barrier, len(partners))
    pred_copies = []
    for c in range(NCH):
        chunk = []
        for j in range(1, MEMBERS):
            to = (m + j) % MEMBERS
            copy = remote(psrc.at[c, to], prcv.at[c, m], psem.at[c], j, member_dev(to))
            copy.start()
            chunk.append(copy)
        pred_copies.append(chunk)

    gbuf[:, VS:VP, :] = jnp.zeros((NCH * MEMBERS, VP - VS, 128), BF)
    gout[...] = jnp.zeros_like(gout)
    woT[...] = jnp.zeros_like(woT)
    woT[0:V, :] = wout_t[...]
    rows_at = lax.broadcasted_iota(jnp.int32, (V, V), 0)
    cols_at = lax.broadcasted_iota(jnp.int32, (V, V), 1)
    vcol = jnp.sum(jnp.where(rows_at == cols_at, jnp.broadcast_to(vw[...], (V, V)), 0.0), axis=1, keepdims=True)
    win_copy.wait()
    lax.fori_loop(0, steps, forward, 0)

    grad_copies = []
    for c in range(NCH):
        own_copies[2 * c].wait()
        own_copies[2 * c + 1].wait()
        for copy in pred_copies[c]:
            copy.wait_recv()
        cols = pl.ds(pl.multiple_of(c * half + 128 * m, 128), 128)
        weight = vcol * area[:, cols]
        rounded = weight.astype(BF).astype(F32)
        aim = tgt[c].astype(F32)
        preds = [prcv[c, k].astype(F32) for k in range(MEMBERS)]
        counts = [None] * MEMBERS
        for i in range(MEMBERS):
            for k in range(i):
                s = jnp.where(preds[i] > preds[k], 1.0, jnp.where(preds[i] < preds[k], -1.0, 0.0))
                counts[i] = s if counts[i] is None else counts[i] + s
                counts[k] = -s if counts[k] is None else counts[k] - s
        for k in range(MEMBERS):
            s = jnp.where(preds[k] > aim, 1.0, jnp.where(preds[k] < aim, -1.0, 0.0))
            grad = weight * s / MEMBERS - (rounded * counts[k]) / (MEMBERS * (MEMBERS - 1))
            gout[c, k, :V, :] = grad.astype(BF)
        chunk = []
        for j in range(1, MEMBERS):
            to = (m + j) % MEMBERS
            copy = remote(gout.at[c, to], gbuf.at[c * MEMBERS + m, pl.ds(0, VS)], gsem.at[c], j, member_dev(to))
            copy.start()
            chunk.append(copy)
        gbuf[c * MEMBERS + m, 0:VS, :] = gout[c, m]
        grad_copies.append(chunk)

    def back(i, carry):
        rows = pl.ds(pl.multiple_of(i * 128, 128), 128)
        turned = jnp.transpose(gbuf[i])
        for n in range(0, width, 512):
            pg[rows, n:n + 512] = (dot(turned, woT[:, n:n + 512]) * gp[rows, n:n + 512]).astype(BF)
        return carry

    def hidden_step(i, carry):
        rows = pl.ds(pl.multiple_of(i * BLK, BLK), BLK)
        for n in range(0, width, 256):
            hgs[0, rows, n:n + 256] = dot_nt(pg[rows, :], win[n:n + 256, :]).astype(BF)
        return carry

    other = 1 - core
    sibling = dev(x, y, z, other)
    last = NCH - 1

    def in_tiles(c, which, b):
        for mm in range(0, width // 2, 256):
            for n in range(0, WB, 256):
                yield mm, n, dot(
                    hT[which, mm:mm + 256, c * half:(c + 1) * half],
                    pg[c * half:(c + 1) * half, b * WB + n:b * WB + n + 256],
                )

    def out_rows(c):
        blocks = [gbuf[c * MEMBERS + k] for k in range(MEMBERS)]
        return dot(jnp.concatenate(blocks, axis=1), act[c * half:(c + 1) * half, :])

    for c in range(NCH):
        for copy in grad_copies[c]:
            copy.wait_recv()
        lax.fori_loop(c * MEMBERS, (c + 1) * MEMBERS, back, 0)
        if c == last:
            break
        for which in range(2):
            for b in range(NWB):
                for mm, n, value in in_tiles(c, which, b):
                    if c > 0:
                        value = value + acc[which, b, mm:mm + 256, n:n + 256]
                    acc[which, b, mm:mm + 256, n:n + 256] = value
        oacc[...] = out_rows(c) if c == 0 else oacc[...] + out_rows(c)

    core_copies = []
    for b in range(NWB):
        for mm, n, value in in_tiles(last, other, b):
            value = value + acc[other, b, mm:mm + 256, n:n + 256]
            csnd[b, mm:mm + 256, n:n + 256] = value.astype(BF)
        copy = remote(csnd.at[b], crcv.at[b], csem, b, sibling)
        copy.start()
        core_copies.append(copy)
    out_term = oacc[...] + out_rows(last)
    for h8 in range(width // 128):
        turned = jnp.transpose(out_term[:, h8 * 128:h8 * 128 + 128])
        for q in range(4):
            zl, cc = (h8 % 2) * 2 + q // 2, q % 2
            first = (h8 // 2) * 128 + zl * 32
            oown[cc, first:first + 32, :] = turned[q * 32:q * 32 + 32, :]
    cosnd[...] = oown[other].astype(BF)
    copy = remote(cosnd, corcv, csem, NWB, sibling)
    copy.start()
    core_copies.append(copy)

    x1, y1, o1 = [], [], []
    for b in range(NWB):
        for mm, n, value in in_tiles(last, core, b):
            acc[core, b, mm:mm + 256, n:n + 256] = value + acc[core, b, mm:mm + 256, n:n + 256]
        core_copies[b].wait_recv()
        for q in range(4):
            rows = slice(q * 128, q * 128 + 128)
            total = acc[core, b, rows, :] + crcv[b, rows, :].astype(F32)
            acc[core, b, rows, :] = total
            s1[b, q] = total.astype(BF)
        for j in (1, 2, 3):
            xx, yy = (x + j) % 4, (y + j) % 4
            copy = remote(s1.at[b, xx, pl.ds(0, 64)], r1a.at[b, x], x1sem.at[b], j, dev(xx, y, z, core))
            copy.start()
            x1.append(copy)
            cols = pl.ds(pl.multiple_of(yy * 128, 128), 128)
            copy = remote(s1.at[b, :, pl.ds(64, 64), cols], r1b.at[b, y], y1sem.at[b], j, dev(x, yy, z, core))
            copy.start()
            y1.append(copy)
    core_copies[NWB].wait_recv()
    for q in range(4):
        rows = slice(q * 128, q * 128 + 128)
        total = oown[core, rows, :] + corcv[rows, :].astype(F32)
        oown[core, rows, :] = total
        s1o[q] = total.astype(BF)
    for j in (1, 2, 3):
        xx = (x + j) % 4
        copy = remote(s1o.at[xx], r1o.at[x], o1sem, j, dev(xx, y, z, core))
        copy.start()
        o1.append(copy)

    per = steps // 2
    lax.fori_loop(0, per, hidden_step, 0)

    own_cols = pl.ds(pl.multiple_of(y * 128, 128), 128)
    own_x = pl.multiple_of(x * 128, 128)
    for copy in x1 + y1 + o1:
        copy.wait_recv()
    for b in range(NWB):
        ta = acc[core, b, pl.ds(own_x, 64), :]
        for j in (1, 2, 3):
            ta = ta + r1a[b, (x + j) % 4].astype(F32)
        a2[b] = ta
        for q in range(4):
            tb = acc[core, b, q * 128 + 64:q * 128 + 128, own_cols]
            for j in (1, 2, 3):
                tb = tb + r1b[b, (y + j) % 4, q].astype(F32)
            b2[b, q] = tb
            s2a[q, 64 * b:64 * b + 64, :] = ta[:, q * 128:q * 128 + 128].astype(BF)
            s2b[q, 64 * b:64 * b + 64, :] = tb.astype(BF)
    to = oown[core, pl.ds(own_x, 128), :]
    for j in (1, 2, 3):
        to = to + r1o[(x + j) % 4].astype(F32)
    for q in range(4):
        part = jnp.concatenate([to[zl * 32 + q * 8:zl * 32 + q * 8 + 8, :] for zl in range(4)], axis=0)
        oown[core, q * 32:q * 32 + 32, :] = part
        s2a[q, 128:160, :] = part.astype(BF)
    second = []
    for j in (1, 2, 3):
        xx, yy = (x + j) % 4, (y + j) % 4
        copy = remote(s2a.at[yy], r2a.at[y], a2sem, j, dev(x, yy, z, core))
        copy.start()
        second.append(copy)
        copy = remote(s2b.at[xx], r2b.at[x], b2sem, j, dev(xx, y, z, core))
        copy.start()
        second.append(copy)
    lax.fori_loop(per, steps, hidden_step, 0)
    for copy in second:
        copy.wait_recv()

    empty = jnp.zeros((8, 128), F32)
    to = oown[core, pl.ds(pl.multiple_of(y * 32, 32), 32), :]
    for j in (1, 2, 3):
        to = to + r2a[(y + j) % 4, 128:160, :].astype(F32)
    sums = []
    for b in range(NWB):
        ta = a2[b, :, own_cols]
        tb = b2[b, x]
        for j in (1, 2, 3):
            ta = ta + r2a[(y + j) % 4, 64 * b:64 * b + 64, :].astype(F32)
            tb = tb + r2b[(x + j) % 4, 64 * b:64 * b + 64, :].astype(F32)
        sums.append((ta[0:32], ta[32:64], tb[0:32], tb[32:64]))
    for q in range(4):
        part = jnp.concatenate([sums[0][q], sums[1][q], to[q * 8:q * 8 + 8, :], empty], axis=0)
        z4[q] = part
        s3[q] = part.astype(BF)
    third = []
    for j in range(1, 8):
        zz = (z + j) % 8
        copy = remote(s3.at[zz % 4], r3.at[z], z3sem, j, dev(x, y, zz, core))
        copy.start()
        third.append(copy)
    total = z4[z_lo]
    for copy in third:
        copy.wait_recv()
    for j in range(1, 8):
        total = total + r3[(z + j) % 8].astype(F32)
    total = total * scale
    s4[...] = total.astype(BF)

    fourth = []
    for j in (1, 2, 3):
        copy = remote(s4, r4.at[y], y4sem, j, dev(x, (y + j) % 4, z, core))
        copy.start()
        fourth.append(copy)
    r4[y] = s4[...]
    for chunk in pred_copies + grad_copies:
        for copy in chunk:
            copy.wait_send()
    for copy in core_copies + x1 + y1 + o1 + second + third:
        copy.wait_send()
    for copy in fourth:
        copy.wait_recv()
    for q in range(4):
        got = r4[q].astype(F32)
        for b in range(NWB):
            win_out[:, b * WB + q * 128:b * WB + q * 128 + 128] = got[32 * b:32 * b + 32, :]
        wout_out[q * 8:q * 8 + 8, :] = got[64:72, 0:V]
    for copy in fourth:
        copy.wait_send()


def place(hg_in, in_in, out_in, hg_out, in_out, out_out, sem):
    points = hg_in.shape[1]
    parts = 4
    copies = []
    for i in range(parts):
        rows = pl.ds(i * (points // parts), points // parts)
        copies.append(pltpu.make_async_copy(hg_in.at[0, rows], hg_out.at[0, rows], sem.at[i]))
    copies.append(pltpu.make_async_copy(in_in, in_out, sem.at[parts]))
    copies.append(pltpu.make_async_copy(out_in, out_out, sem.at[parts + 1]))
    for copy in copies:
        copy.start()
    for copy in copies:
        copy.wait()


def shards(hidden, pred, target, area, var_weight, w_in, w_out):
    points, width = hidden.shape[1:]
    scale = 1.0 / math.sqrt(points * lax.axis_size("grid") * MEMBERS)
    share = width // lax.axis_size("grid")
    any_spec = pl.BlockSpec(memory_space=pl.ANY)
    vmem_spec = pl.BlockSpec(memory_space=pltpu.VMEM)

    def vm(*shape, dtype=BF):
        return pltpu.VMEM(shape, dtype)

    def sems(*shape):
        return pltpu.SemaphoreType.DMA(shape)

    out_types = (
        jax.ShapeDtypeStruct(hidden.shape, BF),
        jax.ShapeDtypeStruct((share, width), F32),
        jax.ShapeDtypeStruct((share, V), F32),
    )
    half = width // 2
    results = pl.pallas_call(
        functools.partial(kernel, scale),
        out_shape=tuple(pltpu.VMEM(t.shape, t.dtype) for t in out_types),
        in_specs=[any_spec, any_spec, any_spec, vmem_spec, vmem_spec, any_spec, vmem_spec],
        out_specs=(vmem_spec, vmem_spec, vmem_spec),
        scratch_shapes=[
            vm(points, width), vm(width, width), vm(2, half, points), vm(points, width),
            vm(points, width, dtype=F32), vm(points, width), vm(VP, width),
            vm(NCH, MEMBERS, V, 128), vm(NCH, MEMBERS, V, 128), vm(NCH, V, 128), vm(NCH, MEMBERS, VS, 128),
            vm(NCH * MEMBERS, VP, 128),
            vm(2, NWB, half, WB, dtype=F32), vm(NWB, half, WB), vm(NWB, half, WB),
            vm(VP, width, dtype=F32), vm(half, VP), vm(half, VP), vm(2, half, VP, dtype=F32),
            vm(NWB, 4, 128, WB), vm(4, 128, VP), vm(NWB, 4, 64, WB), vm(NWB, 4, 4, 64, 128), vm(4, 128, VP),
            vm(NWB, 64, WB, dtype=F32), vm(NWB, 4, 64, 128, dtype=F32),
            vm(4, 160, 128), vm(4, 128, 128), vm(4, 160, 128), vm(4, 128, 128),
            vm(4, 80, 128, dtype=F32), vm(4, 80, 128), vm(8, 80, 128), vm(80, 128), vm(4, 80, 128),
            sems(3 + MEMBERS, NCH), sems(points // BLK),
            sems(NCH, 2, MEMBERS), sems(NCH, 2, MEMBERS), sems(2, NWB + 1),
            sems(NWB, 2, 4), sems(NWB, 2, 4), sems(2, 4), sems(2, 4), sems(2, 4), sems(2, 8), sems(2, 4),
        ],
        compiler_params=pltpu.CompilerParams(
            collective_id=0, has_side_effects=True, vmem_limit_bytes=50 * 1024 * 1024
        ),
    )(hidden, pred, target, area.reshape(1, -1), var_weight.reshape(1, -1), w_in, w_out.T)
    return pl.pallas_call(
        place,
        out_shape=out_types,
        in_specs=[vmem_spec] * 3,
        out_specs=(any_spec,) * 3,
        scratch_shapes=[sems(6)],
        compiler_params=pltpu.CompilerParams(vmem_limit_bytes=8 * 1024 * 1024),
    )(*results)


def solution(mesh):
    return jax.shard_map(
        shards,
        mesh=mesh,
        in_specs=(
            P("member", "grid", None),
            P("member", None, "grid"),
            P(None, "grid"),
            P("grid"),
            P(),
            P(),
            P(),
        ),
        out_specs=(P("member", "grid", None), P("grid", None), P("grid", None)),
        check_vma=False,
    )
```

```python
import functools
import math

import jax
import jax.numpy as jnp
from jax import lax
from jax.experimental import pallas as pl
from jax.experimental.pallas import tpu as pltpu
from jax.sharding import PartitionSpec as P

BF = jnp.bfloat16
F32 = jnp.float32
MEMBERS = 8
V = 100
VS = 112
VP = 128
NCH = 2
BLK = 512
HB = 1024
GB = 4
WB = 512
NWB = 2
ROOT = math.sqrt(2.0 / math.pi)


def dot(a, b):
    return jnp.dot(a, b, preferred_element_type=F32)


def dot_nt(a, b):
    return lax.dot_general(a, b, (((1,), (1,)), ((), ())), preferred_element_type=F32)


def kernel(
    scale,
    hid_hbm, pred_hbm, tgt_hbm, area, vw, win_hbm, wout_t,
    hgs, win_out, wout_out,
    hid, win, hT, act, gp, pg, woT,
    psrc, prcv, tgt, gout, gbuf,
    acc, csnd, crcv, oacc, cosnd, corcv, oown,
    s1, s1o, r1a, r1b, r1o, a2, b2,
    s2a, s2b, r2a, r2b, z4, s3, r3, s4, r4,
    lsem, hsem, psem, gsem, csem, x1sem, y1sem, o1sem, a2sem, b2sem, z3sem, y4sem,
):
    points = hid.shape[0]
    width = hid.shape[1]
    half = points // NCH
    m = lax.axis_index("member")
    g = lax.axis_index("grid")
    y, z_hi = m // 2, m % 2
    x, z_lo, core = g // 8, (g // 2) % 4, g % 2
    z = z_hi * 4 + z_lo

    def dev(xx, yy, zz, cc):
        return (yy * 2 + zz // 4, (xx * 4 + zz % 4) * 2 + cc)

    def member_dev(mm):
        return (mm, g)

    def remote(src, dst, sems, j, target):
        return pltpu.make_async_remote_copy(
            src_ref=src, dst_ref=dst, send_sem=sems.at[0, j], recv_sem=sems.at[1, j],
            device_id=target, device_id_type=pl.DeviceIdType.MESH,
        )

    members_far_first = [
        (1 + k, 2 * ((y + dy) % 4) + (z_hi + dz) % 2)
        for k, (dy, dz) in enumerate(((2, 1), (1, 1), (3, 1), (0, 1), (2, 0), (1, 0), (3, 0)))
    ]

    barrier = pltpu.get_barrier_semaphore()
    partners = [member_dev(to) for _, to in members_far_first]
    partners += [dev(x, y, (z + j) % 8, core) for j in (3, 5, 2, 6, 1, 7)]
    partners += [dev((x + j) % 4, y, z, core) for j in (1, 2, 3)]
    partners += [dev(x, y, z, 1 - core)]
    for partner in partners:
        pl.semaphore_signal(barrier, inc=1, device_id=partner, device_id_type=pl.DeviceIdType.MESH)

    win_copy = pltpu.make_async_copy(win_hbm, win, lsem.at[0, 0])
    win_copy.start()

    def hid_copy(i):
        rows = pl.ds(pl.multiple_of(i * BLK, BLK), BLK)
        return pltpu.make_async_copy(hid_hbm.at[0, rows], hid.at[rows], hsem.at[i])

    own_copies, source_copies = [], []
    for c in range(NCH):
        mine = pl.ds(pl.multiple_of(c * half + 128 * m, 128), 128)
        own_copies.append(pltpu.make_async_copy(pred_hbm.at[0, :, mine], prcv.at[c, m], lsem.at[1, c]))
        own_copies.append(pltpu.make_async_copy(tgt_hbm.at[:, mine], tgt.at[c], lsem.at[2, c]))
        for k in range(MEMBERS):
            cols = pl.ds(c * half + 128 * k, 128)
            source_copies.append(pltpu.make_async_copy(pred_hbm.at[0, :, cols], psrc.at[c, k], lsem.at[3 + k, c]))
    for copy in source_copies + own_copies:
        copy.start()
    hid_copy(0).start()
    for i in range(1, points // BLK):
        hid_copy(i).start()


    def forward(i, carry):
        hid_copy(i).wait()
        rows = pl.ds(pl.multiple_of(i * BLK, BLK), BLK)
        h = hid[rows, :]
        for n in range(0, width, 256):
            u = dot(h, win[:, n:n + 256])
            square = u * u
            t = jnp.tanh(u * (square * (ROOT * 0.044715) + ROOT))
            p = 0.5 * t + 0.5
            a = u * p
            act[rows, n:n + 256] = a.astype(BF)
            gp[rows, n:n + 256] = p + (a * (1.0 - p)) * (square * (ROOT * 0.044715 * 6.0) + 2.0 * ROOT)
        for t8 in range(width // 128):
            turned = jnp.transpose(h[:, t8 * 128:t8 * 128 + 128])
            for q in range(4):
                zl, cc = (t8 % 2) * 2 + q // 2, q % 2
                first = (t8 // 2) * 128 + zl * 32
                hT[cc, first:first + 32, rows] = turned[q * 32:q * 32 + 32, :]
        return carry

    steps = points // BLK

    for copy in source_copies:
        copy.wait()
    pl.semaphore_wait(barrier, len(partners))
    pred_copies = []
    for c in range(NCH):
        chunk = []
        for j, to in members_far_first:
            copy = remote(psrc.at[c, to], prcv.at[c, m], psem.at[c], j, member_dev(to))
            copy.start()
            chunk.append(copy)
        pred_copies.append(chunk)

    gbuf[:, VS:VP, :] = jnp.zeros((NCH * MEMBERS, VP - VS, 128), BF)
    gout[...] = jnp.zeros_like(gout)
    woT[...] = jnp.zeros_like(woT)
    woT[0:V, :] = wout_t[...]
    rows_at = lax.broadcasted_iota(jnp.int32, (V, V), 0)
    cols_at = lax.broadcasted_iota(jnp.int32, (V, V), 1)
    vcol = jnp.sum(jnp.where(rows_at == cols_at, jnp.broadcast_to(vw[...], (V, V)), 0.0), axis=1, keepdims=True)
    win_copy.wait()
    lax.fori_loop(0, steps, forward, 0)

    grad_copies = []
    for c in range(NCH):
        own_copies[2 * c].wait()
        own_copies[2 * c + 1].wait()
        for copy in pred_copies[c]:
            copy.wait_recv()
        cols = pl.ds(pl.multiple_of(c * half + 128 * m, 128), 128)
        weight = vcol * area[:, cols]
        rounded = weight.astype(BF).astype(F32)
        aim = tgt[c].astype(F32)
        preds = [prcv[c, k].astype(F32) for k in range(MEMBERS)]
        counts = [None] * MEMBERS
        for i in range(MEMBERS):
            for k in range(i):
                s = jnp.where(preds[i] > preds[k], 1.0, jnp.where(preds[i] < preds[k], -1.0, 0.0))
                counts[i] = s if counts[i] is None else counts[i] + s
                counts[k] = -s if counts[k] is None else counts[k] - s
        for k in range(MEMBERS):
            s = jnp.where(preds[k] > aim, 1.0, jnp.where(preds[k] < aim, -1.0, 0.0))
            grad = weight * s / MEMBERS - (rounded * counts[k]) / (MEMBERS * (MEMBERS - 1))
            gout[c, k, :V, :] = grad.astype(BF)
        chunk = []
        for j, to in members_far_first:
            copy = remote(gout.at[c, to], gbuf.at[c * MEMBERS + m, pl.ds(0, VS)], gsem.at[c], j, member_dev(to))
            copy.start()
            chunk.append(copy)
        gbuf[c * MEMBERS + m, 0:VS, :] = gout[c, m]
        grad_copies.append(chunk)

    def back(i, carry):
        rows = pl.ds(pl.multiple_of(i * (GB * 128), GB * 128), GB * 128)
        turned = jnp.concatenate([jnp.transpose(gbuf[i * GB + k]) for k in range(GB)], axis=0)
        for n in range(0, width, 512):
            pg[rows, n:n + 512] = (dot(turned, woT[:, n:n + 512]) * gp[rows, n:n + 512]).astype(BF)
        return carry

    def hidden_step(i, carry):
        rows = pl.ds(pl.multiple_of(i * HB, HB), HB)
        for n in range(0, width, 256):
            hgs[0, rows, n:n + 256] = dot_nt(pg[rows, :], win[n:n + 256, :]).astype(BF)
        return carry

    other = 1 - core
    sibling = dev(x, y, z, other)
    last = NCH - 1

    def in_tiles(c, which, b):
        for n in range(0, WB, 256):
            yield slice(n, n + 256), dot(
                hT[which, :, c * half:(c + 1) * half],
                pg[c * half:(c + 1) * half, b * WB + n:b * WB + n + 256],
            )

    def out_rows(c):
        blocks = [gbuf[c * MEMBERS + k] for k in range(MEMBERS)]
        return dot(jnp.concatenate(blocks, axis=1), act[c * half:(c + 1) * half, :])

    for c in range(NCH):
        for copy in grad_copies[c]:
            copy.wait_recv()
        lax.fori_loop(c * (MEMBERS // GB), (c + 1) * (MEMBERS // GB), back, 0)
        if c == last:
            break
        for which in range(2):
            for b in range(NWB):
                for cols, value in in_tiles(c, which, b):
                    acc[which, b, :, cols] = value if c == 0 else value + acc[which, b, :, cols]
        oacc[...] = out_rows(c) if c == 0 else oacc[...] + out_rows(c)

    core_copies = []
    for b in range(NWB):
        for cols, value in in_tiles(last, other, b):
            csnd[b, :, cols] = (value + acc[other, b, :, cols]).astype(BF)
        copy = remote(csnd.at[b], crcv.at[b], csem, b, sibling)
        copy.start()
        core_copies.append(copy)
    x1, y1, o1 = [], [], []
    for b in range(NWB):
        for cols, value in in_tiles(last, core, b):
            acc[core, b, :, cols] = value + acc[core, b, :, cols]
        core_copies[b].wait_recv()
        for q in range(4):
            rows = slice(q * 128, q * 128 + 128)
            total = acc[core, b, rows, :] + crcv[b, rows, :].astype(F32)
            acc[core, b, rows, :] = total
            s1[b, q] = total.astype(BF)
        for j in (1, 2, 3):
            xx, yy = (x + j) % 4, (y + j) % 4
            copy = remote(s1.at[b, xx, pl.ds(0, 64)], r1a.at[b, x], x1sem.at[b], j, dev(xx, y, z, core))
            copy.start()
            x1.append(copy)
            cols = pl.ds(pl.multiple_of(yy * 128, 128), 128)
            copy = remote(s1.at[b, :, pl.ds(64, 64), cols], r1b.at[b, y], y1sem.at[b], j, dev(x, yy, z, core))
            copy.start()
            y1.append(copy)
    out_term = oacc[...] + out_rows(last)
    for h8 in range(width // 128):
        turned = jnp.transpose(out_term[:, h8 * 128:h8 * 128 + 128])
        for q in range(4):
            zl, cc = (h8 % 2) * 2 + q // 2, q % 2
            first = (h8 // 2) * 128 + zl * 32
            oown[cc, first:first + 32, :] = turned[q * 32:q * 32 + 32, :]
    cosnd[...] = oown[other].astype(BF)
    copy = remote(cosnd, corcv, csem, NWB, sibling)
    copy.start()
    core_copies.append(copy)

    core_copies[NWB].wait_recv()
    for q in range(4):
        rows = slice(q * 128, q * 128 + 128)
        total = oown[core, rows, :] + corcv[rows, :].astype(F32)
        oown[core, rows, :] = total
        s1o[q] = total.astype(BF)
    for j in (1, 2, 3):
        xx = (x + j) % 4
        copy = remote(s1o.at[xx], r1o.at[x], o1sem, j, dev(xx, y, z, core))
        copy.start()
        o1.append(copy)

    per = points // HB // 2
    lax.fori_loop(0, per, hidden_step, 0)

    own_cols = pl.ds(pl.multiple_of(y * 128, 128), 128)
    own_x = pl.multiple_of(x * 128, 128)
    for copy in x1 + y1 + o1:
        copy.wait_recv()
    for b in range(NWB):
        ta = acc[core, b, pl.ds(own_x, 64), :]
        for j in (1, 2, 3):
            ta = ta + r1a[b, (x + j) % 4].astype(F32)
        a2[b] = ta
        for q in range(4):
            tb = acc[core, b, q * 128 + 64:q * 128 + 128, own_cols]
            for j in (1, 2, 3):
                tb = tb + r1b[b, (y + j) % 4, q].astype(F32)
            b2[b, q] = tb
            s2a[q, 64 * b:64 * b + 64, :] = ta[:, q * 128:q * 128 + 128].astype(BF)
            s2b[q, 64 * b:64 * b + 64, :] = tb.astype(BF)
    to = oown[core, pl.ds(own_x, 128), :]
    for j in (1, 2, 3):
        to = to + r1o[(x + j) % 4].astype(F32)
    for q in range(4):
        part = jnp.concatenate([to[zl * 32 + q * 8:zl * 32 + q * 8 + 8, :] for zl in range(4)], axis=0)
        oown[core, q * 32:q * 32 + 32, :] = part
        s2a[q, 128:160, :] = part.astype(BF)
    second = []
    for j in (1, 2, 3):
        xx, yy = (x + j) % 4, (y + j) % 4
        copy = remote(s2a.at[yy], r2a.at[y], a2sem, j, dev(x, yy, z, core))
        copy.start()
        second.append(copy)
        copy = remote(s2b.at[xx], r2b.at[x], b2sem, j, dev(xx, y, z, core))
        copy.start()
        second.append(copy)
    lax.fori_loop(per, 2 * per, hidden_step, 0)
    for copy in second:
        copy.wait_recv()

    empty = jnp.zeros((8, 128), F32)
    to = oown[core, pl.ds(pl.multiple_of(y * 32, 32), 32), :]
    for j in (1, 2, 3):
        to = to + r2a[(y + j) % 4, 128:160, :].astype(F32)
    sums = []
    for b in range(NWB):
        ta = a2[b, :, own_cols]
        tb = b2[b, x]
        for j in (1, 2, 3):
            ta = ta + r2a[(y + j) % 4, 64 * b:64 * b + 64, :].astype(F32)
            tb = tb + r2b[(x + j) % 4, 64 * b:64 * b + 64, :].astype(F32)
        sums.append((ta[0:32], ta[32:64], tb[0:32], tb[32:64]))
    for q in range(4):
        part = jnp.concatenate([sums[0][q], sums[1][q], to[q * 8:q * 8 + 8, :], empty], axis=0)
        z4[q] = part
        s3[q] = part.astype(BF)
    third = []
    for j in (4, 3, 5, 2, 6, 1, 7):
        zz = (z + j) % 8
        copy = remote(s3.at[zz % 4], r3.at[z], z3sem, j, dev(x, y, zz, core))
        copy.start()
        third.append(copy)
    total = z4[z_lo]
    for copy in third:
        copy.wait_recv()
    for j in range(1, 8):
        total = total + r3[(z + j) % 8].astype(F32)
    total = total * scale
    s4[...] = total.astype(BF)

    fourth = []
    for j in (1, 2, 3):
        copy = remote(s4, r4.at[y], y4sem, j, dev(x, (y + j) % 4, z, core))
        copy.start()
        fourth.append(copy)
    r4[y] = s4[...]
    for chunk in pred_copies + grad_copies:
        for copy in chunk:
            copy.wait_send()
    for copy in core_copies + x1 + y1 + o1 + second + third:
        copy.wait_send()
    for copy in fourth:
        copy.wait_recv()
    for q in range(4):
        got = r4[q].astype(F32)
        for b in range(NWB):
            win_out[:, b * WB + q * 128:b * WB + q * 128 + 128] = got[32 * b:32 * b + 32, :]
        wout_out[q * 8:q * 8 + 8, :] = got[64:72, 0:V]
    for copy in fourth:
        copy.wait_send()


def place(hg_in, in_in, out_in, hg_out, in_out, out_out, sem):
    points = hg_in.shape[1]
    parts = 8
    copies = []
    for i in range(parts):
        rows = pl.ds(i * (points // parts), points // parts)
        copies.append(pltpu.make_async_copy(hg_in.at[0, rows], hg_out.at[0, rows], sem.at[i]))
    copies.append(pltpu.make_async_copy(in_in, in_out, sem.at[parts]))
    copies.append(pltpu.make_async_copy(out_in, out_out, sem.at[parts + 1]))
    for copy in copies:
        copy.start()
    for copy in copies:
        copy.wait()


def shards(hidden, pred, target, area, var_weight, w_in, w_out):
    points, width = hidden.shape[1:]
    scale = 1.0 / math.sqrt(points * lax.axis_size("grid") * MEMBERS)
    share = width // lax.axis_size("grid")
    any_spec = pl.BlockSpec(memory_space=pl.ANY)
    vmem_spec = pl.BlockSpec(memory_space=pltpu.VMEM)

    def vm(*shape, dtype=BF):
        return pltpu.VMEM(shape, dtype)

    def sems(*shape):
        return pltpu.SemaphoreType.DMA(shape)

    out_types = (
        jax.ShapeDtypeStruct(hidden.shape, BF),
        jax.ShapeDtypeStruct((share, width), F32),
        jax.ShapeDtypeStruct((share, V), F32),
    )
    half = width // 2
    results = pl.pallas_call(
        functools.partial(kernel, scale),
        out_shape=tuple(pltpu.VMEM(t.shape, t.dtype) for t in out_types),
        in_specs=[any_spec, any_spec, any_spec, vmem_spec, vmem_spec, any_spec, vmem_spec],
        out_specs=(vmem_spec, vmem_spec, vmem_spec),
        scratch_shapes=[
            vm(points, width), vm(width, width), vm(2, half, points), vm(points, width),
            vm(points, width, dtype=F32), vm(points, width), vm(VP, width),
            vm(NCH, MEMBERS, V, 128), vm(NCH, MEMBERS, V, 128), vm(NCH, V, 128), vm(NCH, MEMBERS, VS, 128),
            vm(NCH * MEMBERS, VP, 128),
            vm(2, NWB, half, WB, dtype=F32), vm(NWB, half, WB), vm(NWB, half, WB),
            vm(VP, width, dtype=F32), vm(half, VP), vm(half, VP), vm(2, half, VP, dtype=F32),
            vm(NWB, 4, 128, WB), vm(4, 128, VP), vm(NWB, 4, 64, WB), vm(NWB, 4, 4, 64, 128), vm(4, 128, VP),
            vm(NWB, 64, WB, dtype=F32), vm(NWB, 4, 64, 128, dtype=F32),
            vm(4, 160, 128), vm(4, 128, 128), vm(4, 160, 128), vm(4, 128, 128),
            vm(4, 80, 128, dtype=F32), vm(4, 80, 128), vm(8, 80, 128), vm(80, 128), vm(4, 80, 128),
            sems(3 + MEMBERS, NCH), sems(points // BLK),
            sems(NCH, 2, MEMBERS), sems(NCH, 2, MEMBERS), sems(2, NWB + 1),
            sems(NWB, 2, 4), sems(NWB, 2, 4), sems(2, 4), sems(2, 4), sems(2, 4), sems(2, 8), sems(2, 4),
        ],
        compiler_params=pltpu.CompilerParams(
            collective_id=0, has_side_effects=True, vmem_limit_bytes=50 * 1024 * 1024
        ),
    )(hidden, pred, target, area.reshape(1, -1), var_weight.reshape(1, -1), w_in, w_out.T)
    return pl.pallas_call(
        place,
        out_shape=out_types,
        in_specs=[vmem_spec] * 3,
        out_specs=(any_spec,) * 3,
        scratch_shapes=[sems(10)],
        compiler_params=pltpu.CompilerParams(vmem_limit_bytes=8 * 1024 * 1024),
    )(*results)


def solution(mesh):
    return jax.shard_map(
        shards,
        mesh=mesh,
        in_specs=(
            P("member", "grid", None),
            P("member", None, "grid"),
            P(None, "grid"),
            P("grid"),
            P(),
            P(),
            P(),
        ),
        out_specs=(P("member", "grid", None), P("grid", None), P("grid", None)),
        check_vma=False,
    )
```

```python
import functools
import math

import jax
import jax.numpy as jnp
from jax import lax
from jax.experimental import pallas as pl
from jax.experimental.pallas import tpu as pltpu
from jax.sharding import PartitionSpec as P

BF = jnp.bfloat16
F32 = jnp.float32
MEMBERS = 8
V = 100
VS = 112
VP = 128
NCH = 2
BLK = 512
HB = 1024
GB = 4
WB = 512
NWB = 2
ROOT = math.sqrt(2.0 / math.pi)


def dot(a, b):
    return jnp.dot(a, b, preferred_element_type=F32)


def dot_nt(a, b):
    return lax.dot_general(a, b, (((1,), (1,)), ((), ())), preferred_element_type=F32)


def kernel(
    scale,
    hid_hbm, pred_hbm, tgt_hbm, area, vw, win_hbm, wout_t,
    hgs, win_out, wout_out,
    hid, win, hT, act, gp, pg, woT,
    psrc, prcv, tgt, gout, gbuf,
    acc, csnd, crcv, oacc, cosnd, corcv, oown,
    s1, s1o, r1a, r1b, r1o, a2, b2,
    s2a, s2b, r2a, r2b, z4, s3, r3, s4, r4,
    lsem, hsem, psem, gsem, csem, x1sem, y1sem, o1sem, a2sem, b2sem, z3sem, y4sem,
):
    points = hid.shape[0]
    width = hid.shape[1]
    half = points // NCH
    m = lax.axis_index("member")
    g = lax.axis_index("grid")
    y, z_hi = m // 2, m % 2
    x, z_lo, core = g // 8, (g // 2) % 4, g % 2
    z = z_hi * 4 + z_lo

    def dev(xx, yy, zz, cc):
        return (yy * 2 + zz // 4, (xx * 4 + zz % 4) * 2 + cc)

    def member_dev(mm):
        return (mm, g)

    def remote(src, dst, sems, j, target):
        return pltpu.make_async_remote_copy(
            src_ref=src, dst_ref=dst, send_sem=sems.at[0, j], recv_sem=sems.at[1, j],
            device_id=target, device_id_type=pl.DeviceIdType.MESH,
        )

    mine_p = z_hi * 4 + y

    members_far_first = []
    for k, (dy, dz) in enumerate(((2, 1), (1, 1), (3, 1), (0, 1), (2, 0), (1, 0), (3, 0))):
        to_y, to_z = (y + dy) % 4, (z_hi + dz) % 2
        members_far_first.append((1 + k, to_z * 4 + to_y, 2 * to_y + to_z))
    fars = 4

    barrier = pltpu.get_barrier_semaphore()
    partners = [member_dev(to) for _, _, to in members_far_first]
    partners += [dev(x, y, (z + j) % 8, core) for j in (3, 5, 2, 6, 1, 7)]
    partners += [dev((x + j) % 4, y, z, core) for j in (1, 2, 3)]
    partners += [dev(x, y, z, 1 - core)]
    for partner in partners:
        pl.semaphore_signal(barrier, inc=1, device_id=partner, device_id_type=pl.DeviceIdType.MESH)

    win_copy = pltpu.make_async_copy(win_hbm, win, lsem.at[0, 0])
    win_copy.start()

    def hid_copy(i):
        rows = pl.ds(pl.multiple_of(i * BLK, BLK), BLK)
        return pltpu.make_async_copy(hid_hbm.at[0, rows], hid.at[rows], hsem.at[i])

    own_copies, source_copies = [], []
    for c in range(NCH):
        mine = pl.ds(pl.multiple_of(c * half + 128 * mine_p, 128), 128)
        own_copies.append(pltpu.make_async_copy(pred_hbm.at[0, :, mine], prcv.at[c, mine_p], lsem.at[1, c]))
        own_copies.append(pltpu.make_async_copy(tgt_hbm.at[:, mine], tgt.at[c], lsem.at[2, c]))
        for k in range(MEMBERS):
            cols = pl.ds(c * half + 128 * k, 128)
            source_copies.append(pltpu.make_async_copy(pred_hbm.at[0, :, cols], psrc.at[c, k], lsem.at[3 + k, c]))
    for copy in source_copies + own_copies:
        copy.start()
    hid_copy(0).start()
    for i in range(1, points // BLK):
        hid_copy(i).start()


    def forward(i, carry):
        hid_copy(i).wait()
        rows = pl.ds(pl.multiple_of(i * BLK, BLK), BLK)
        h = hid[rows, :]
        for n in range(0, width, 256):
            u = dot(h, win[:, n:n + 256])
            square = u * u
            t = jnp.tanh(u * (square * (ROOT * 0.044715) + ROOT))
            p = 0.5 * t + 0.5
            a = u * p
            act[rows, n:n + 256] = a.astype(BF)
            gp[rows, n:n + 256] = p + (a * (1.0 - p)) * (square * (ROOT * 0.044715 * 6.0) + 2.0 * ROOT)
        for t8 in range(width // 128):
            turned = jnp.transpose(h[:, t8 * 128:t8 * 128 + 128])
            for q in range(4):
                zl, cc = (t8 % 2) * 2 + q // 2, q % 2
                first = (t8 // 2) * 128 + zl * 32
                hT[cc, first:first + 32, rows] = turned[q * 32:q * 32 + 32, :]
        return carry

    steps = points // BLK

    for copy in source_copies:
        copy.wait()
    pl.semaphore_wait(barrier, len(partners))
    pred_copies = []
    for c in range(NCH):
        chunk = []
        for j, p, to in members_far_first:
            copy = remote(psrc.at[c, p], prcv.at[c, mine_p], psem.at[c], j, member_dev(to))
            copy.start()
            chunk.append(copy)
        pred_copies.append(chunk)

    gbuf[:, VS:VP, :] = jnp.zeros((NCH * MEMBERS, VP - VS, 128), BF)
    gout[...] = jnp.zeros_like(gout)
    woT[...] = jnp.zeros_like(woT)
    woT[0:V, :] = wout_t[...]
    rows_at = lax.broadcasted_iota(jnp.int32, (V, V), 0)
    cols_at = lax.broadcasted_iota(jnp.int32, (V, V), 1)
    vcol = jnp.sum(jnp.where(rows_at == cols_at, jnp.broadcast_to(vw[...], (V, V)), 0.0), axis=1, keepdims=True)
    win_copy.wait()
    lax.fori_loop(0, steps, forward, 0)

    grad_copies = []
    for c in range(NCH):
        own_copies[2 * c].wait()
        own_copies[2 * c + 1].wait()
        for copy in pred_copies[c]:
            copy.wait_recv()
        cols = pl.ds(pl.multiple_of(c * half + 128 * mine_p, 128), 128)
        weight = vcol * area[:, cols]
        rounded = weight.astype(BF).astype(F32)
        aim = tgt[c].astype(F32)
        preds = [prcv[c, k].astype(F32) for k in range(MEMBERS)]
        counts = [None] * MEMBERS
        for i in range(MEMBERS):
            for k in range(i):
                s = jnp.where(preds[i] > preds[k], 1.0, jnp.where(preds[i] < preds[k], -1.0, 0.0))
                counts[i] = s if counts[i] is None else counts[i] + s
                counts[k] = -s if counts[k] is None else counts[k] - s
        for k in range(MEMBERS):
            s = jnp.where(preds[k] > aim, 1.0, jnp.where(preds[k] < aim, -1.0, 0.0))
            grad = weight * s / MEMBERS - (rounded * counts[k]) / (MEMBERS * (MEMBERS - 1))
            gout[c, k, :V, :] = grad.astype(BF)
        chunk = []
        for j, p, to in members_far_first:
            copy = remote(gout.at[c, p], gbuf.at[c * MEMBERS + mine_p, pl.ds(0, VS)], gsem.at[c], j, member_dev(to))
            copy.start()
            chunk.append(copy)
        gbuf[c * MEMBERS + mine_p, 0:VS, :] = gout[c, mine_p]
        grad_copies.append(chunk)

    def back(i, carry):
        rows = pl.ds(pl.multiple_of(i * (GB * 128), GB * 128), GB * 128)
        turned = jnp.concatenate([jnp.transpose(gbuf[i * GB + k]) for k in range(GB)], axis=0)
        for n in range(0, width, 512):
            pg[rows, n:n + 512] = (dot(turned, woT[:, n:n + 512]) * gp[rows, n:n + 512]).astype(BF)
        return carry

    def hidden_step(i, carry):
        rows = pl.ds(pl.multiple_of(i * HB, HB), HB)
        for n in range(0, width, 256):
            hgs[0, rows, n:n + 256] = dot_nt(pg[rows, :], win[n:n + 256, :]).astype(BF)
        return carry

    other = 1 - core
    sibling = dev(x, y, z, other)
    last = NCH - 1

    group = GB * 128

    def in_tiles(at, which, b):
        rows = pl.ds(*at)
        for n in range(0, WB, 256):
            yield slice(n, n + 256), dot(hT[which, :, rows], pg[rows, b * WB + n:b * WB + n + 256])

    def out_rows(at, first):
        blocks = [gbuf[first + k] for k in range(at[1] // 128)]
        return dot(jnp.concatenate(blocks, axis=1), act[pl.ds(*at), :])

    def add_terms(at, first, start):
        for which in range(2):
            for b in range(NWB):
                for cols, value in in_tiles(at, which, b):
                    acc[which, b, :, cols] = value if start else value + acc[which, b, :, cols]
        oacc[...] = out_rows(at, first) if start else oacc[...] + out_rows(at, first)

    for c in range(last):
        for copy in grad_copies[c]:
            copy.wait_recv()
        for i in range(MEMBERS // GB):
            back(c * (MEMBERS // GB) + i, 0)
        add_terms((c * half, half), c * MEMBERS, c == 0)

    for copy in grad_copies[last][fars:]:
        copy.wait_recv()
    near = last * 2 + z_hi
    back(near, 0)
    add_terms((pl.multiple_of(near * group, group), group), near * GB, False)
    for copy in grad_copies[last][:fars]:
        copy.wait_recv()
    far = last * 2 + 1 - z_hi
    far_at = (pl.multiple_of(far * group, group), group)
    back(far, 0)

    core_copies = []
    for b in range(NWB):
        for cols, value in in_tiles(far_at, other, b):
            csnd[b, :, cols] = (value + acc[other, b, :, cols]).astype(BF)
        copy = remote(csnd.at[b], crcv.at[b], csem, b, sibling)
        copy.start()
        core_copies.append(copy)
    x1, y1, o1 = [], [], []
    for b in range(NWB):
        for cols, value in in_tiles(far_at, core, b):
            acc[core, b, :, cols] = value + acc[core, b, :, cols]
        core_copies[b].wait_recv()
        for q in range(4):
            rows = slice(q * 128, q * 128 + 128)
            total = acc[core, b, rows, :] + crcv[b, rows, :].astype(F32)
            acc[core, b, rows, :] = total
            s1[b, q] = total.astype(BF)
        for j in (1, 2, 3):
            xx, yy = (x + j) % 4, (y + j) % 4
            copy = remote(s1.at[b, xx, pl.ds(0, 64)], r1a.at[b, x], x1sem.at[b], j, dev(xx, y, z, core))
            copy.start()
            x1.append(copy)
            cols = pl.ds(pl.multiple_of(yy * 128, 128), 128)
            copy = remote(s1.at[b, :, pl.ds(64, 64), cols], r1b.at[b, y], y1sem.at[b], j, dev(x, yy, z, core))
            copy.start()
            y1.append(copy)
    out_term = oacc[...] + out_rows(far_at, far * GB)
    for h8 in range(width // 128):
        turned = jnp.transpose(out_term[:, h8 * 128:h8 * 128 + 128])
        for q in range(4):
            zl, cc = (h8 % 2) * 2 + q // 2, q % 2
            first = (h8 // 2) * 128 + zl * 32
            oown[cc, first:first + 32, :] = turned[q * 32:q * 32 + 32, :]
    cosnd[...] = oown[other].astype(BF)
    copy = remote(cosnd, corcv, csem, NWB, sibling)
    copy.start()
    core_copies.append(copy)

    core_copies[NWB].wait_recv()
    for q in range(4):
        rows = slice(q * 128, q * 128 + 128)
        total = oown[core, rows, :] + corcv[rows, :].astype(F32)
        oown[core, rows, :] = total
        s1o[q] = total.astype(BF)
    for j in (1, 2, 3):
        xx = (x + j) % 4
        copy = remote(s1o.at[xx], r1o.at[x], o1sem, j, dev(xx, y, z, core))
        copy.start()
        o1.append(copy)

    per = points // HB // 2
    lax.fori_loop(0, per, hidden_step, 0)

    own_cols = pl.ds(pl.multiple_of(y * 128, 128), 128)
    own_x = pl.multiple_of(x * 128, 128)
    for copy in x1 + y1 + o1:
        copy.wait_recv()
    for b in range(NWB):
        ta = acc[core, b, pl.ds(own_x, 64), :]
        for j in (1, 2, 3):
            ta = ta + r1a[b, (x + j) % 4].astype(F32)
        a2[b] = ta
        for q in range(4):
            tb = acc[core, b, q * 128 + 64:q * 128 + 128, own_cols]
            for j in (1, 2, 3):
                tb = tb + r1b[b, (y + j) % 4, q].astype(F32)
            b2[b, q] = tb
            s2a[q, 64 * b:64 * b + 64, :] = ta[:, q * 128:q * 128 + 128].astype(BF)
            s2b[q, 64 * b:64 * b + 64, :] = tb.astype(BF)
    to = oown[core, pl.ds(own_x, 128), :]
    for j in (1, 2, 3):
        to = to + r1o[(x + j) % 4].astype(F32)
    for q in range(4):
        part = jnp.concatenate([to[zl * 32 + q * 8:zl * 32 + q * 8 + 8, :] for zl in range(4)], axis=0)
        oown[core, q * 32:q * 32 + 32, :] = part
        s2a[q, 128:160, :] = part.astype(BF)
    second = []
    for j in (1, 2, 3):
        xx, yy = (x + j) % 4, (y + j) % 4
        copy = remote(s2a.at[yy], r2a.at[y], a2sem, j, dev(x, yy, z, core))
        copy.start()
        second.append(copy)
        copy = remote(s2b.at[xx], r2b.at[x], b2sem, j, dev(xx, y, z, core))
        copy.start()
        second.append(copy)
    lax.fori_loop(per, 2 * per, hidden_step, 0)
    for copy in second:
        copy.wait_recv()

    empty = jnp.zeros((8, 128), F32)
    to = oown[core, pl.ds(pl.multiple_of(y * 32, 32), 32), :]
    for j in (1, 2, 3):
        to = to + r2a[(y + j) % 4, 128:160, :].astype(F32)
    sums = []
    for b in range(NWB):
        ta = a2[b, :, own_cols]
        tb = b2[b, x]
        for j in (1, 2, 3):
            ta = ta + r2a[(y + j) % 4, 64 * b:64 * b + 64, :].astype(F32)
            tb = tb + r2b[(x + j) % 4, 64 * b:64 * b + 64, :].astype(F32)
        sums.append((ta[0:32], ta[32:64], tb[0:32], tb[32:64]))
    for q in range(4):
        part = jnp.concatenate([sums[0][q], sums[1][q], to[q * 8:q * 8 + 8, :], empty], axis=0)
        z4[q] = part
        s3[q] = part.astype(BF)
    third = []
    for j in (4, 3, 5, 2, 6, 1, 7):
        zz = (z + j) % 8
        copy = remote(s3.at[zz % 4], r3.at[z], z3sem, j, dev(x, y, zz, core))
        copy.start()
        third.append(copy)
    total = z4[z_lo]
    for copy in third:
        copy.wait_recv()
    for j in range(1, 8):
        total = total + r3[(z + j) % 8].astype(F32)
    total = total * scale
    s4[...] = total.astype(BF)

    fourth = []
    for j in (1, 2, 3):
        copy = remote(s4, r4.at[y], y4sem, j, dev(x, (y + j) % 4, z, core))
        copy.start()
        fourth.append(copy)
    r4[y] = s4[...]
    for chunk in pred_copies + grad_copies:
        for copy in chunk:
            copy.wait_send()
    for copy in core_copies + x1 + y1 + o1 + second + third:
        copy.wait_send()
    for copy in fourth:
        copy.wait_recv()
    for q in range(4):
        got = r4[q].astype(F32)
        for b in range(NWB):
            win_out[:, b * WB + q * 128:b * WB + q * 128 + 128] = got[32 * b:32 * b + 32, :]
        wout_out[q * 8:q * 8 + 8, :] = got[64:72, 0:V]
    for copy in fourth:
        copy.wait_send()


def place(hg_in, in_in, out_in, hg_out, in_out, out_out, sem):
    points = hg_in.shape[1]
    parts = 8
    copies = []
    for i in range(parts):
        rows = pl.ds(i * (points // parts), points // parts)
        copies.append(pltpu.make_async_copy(hg_in.at[0, rows], hg_out.at[0, rows], sem.at[i]))
    copies.append(pltpu.make_async_copy(in_in, in_out, sem.at[parts]))
    copies.append(pltpu.make_async_copy(out_in, out_out, sem.at[parts + 1]))
    for copy in copies:
        copy.start()
    for copy in copies:
        copy.wait()


def shards(hidden, pred, target, area, var_weight, w_in, w_out):
    points, width = hidden.shape[1:]
    scale = 1.0 / math.sqrt(points * lax.axis_size("grid") * MEMBERS)
    share = width // lax.axis_size("grid")
    any_spec = pl.BlockSpec(memory_space=pl.ANY)
    vmem_spec = pl.BlockSpec(memory_space=pltpu.VMEM)

    def vm(*shape, dtype=BF):
        return pltpu.VMEM(shape, dtype)

    def sems(*shape):
        return pltpu.SemaphoreType.DMA(shape)

    out_types = (
        jax.ShapeDtypeStruct(hidden.shape, BF),
        jax.ShapeDtypeStruct((share, width), F32),
        jax.ShapeDtypeStruct((share, V), F32),
    )
    half = width // 2
    results = pl.pallas_call(
        functools.partial(kernel, scale),
        out_shape=tuple(pltpu.VMEM(t.shape, t.dtype) for t in out_types),
        in_specs=[any_spec, any_spec, any_spec, vmem_spec, vmem_spec, any_spec, vmem_spec],
        out_specs=(vmem_spec, vmem_spec, vmem_spec),
        scratch_shapes=[
            vm(points, width), vm(width, width), vm(2, half, points), vm(points, width),
            vm(points, width, dtype=F32), vm(points, width), vm(VP, width),
            vm(NCH, MEMBERS, V, 128), vm(NCH, MEMBERS, V, 128), vm(NCH, V, 128), vm(NCH, MEMBERS, VS, 128),
            vm(NCH * MEMBERS, VP, 128),
            vm(2, NWB, half, WB, dtype=F32), vm(NWB, half, WB), vm(NWB, half, WB),
            vm(VP, width, dtype=F32), vm(half, VP), vm(half, VP), vm(2, half, VP, dtype=F32),
            vm(NWB, 4, 128, WB), vm(4, 128, VP), vm(NWB, 4, 64, WB), vm(NWB, 4, 4, 64, 128), vm(4, 128, VP),
            vm(NWB, 64, WB, dtype=F32), vm(NWB, 4, 64, 128, dtype=F32),
            vm(4, 160, 128), vm(4, 128, 128), vm(4, 160, 128), vm(4, 128, 128),
            vm(4, 80, 128, dtype=F32), vm(4, 80, 128), vm(8, 80, 128), vm(80, 128), vm(4, 80, 128),
            sems(3 + MEMBERS, NCH), sems(points // BLK),
            sems(NCH, 2, MEMBERS), sems(NCH, 2, MEMBERS), sems(2, NWB + 1),
            sems(NWB, 2, 4), sems(NWB, 2, 4), sems(2, 4), sems(2, 4), sems(2, 4), sems(2, 8), sems(2, 4),
        ],
        compiler_params=pltpu.CompilerParams(
            collective_id=0, has_side_effects=True, vmem_limit_bytes=50 * 1024 * 1024
        ),
    )(hidden, pred, target, area.reshape(1, -1), var_weight.reshape(1, -1), w_in, w_out.T)
    return pl.pallas_call(
        place,
        out_shape=out_types,
        in_specs=[vmem_spec] * 3,
        out_specs=(any_spec,) * 3,
        scratch_shapes=[sems(10)],
        compiler_params=pltpu.CompilerParams(vmem_limit_bytes=8 * 1024 * 1024),
    )(*results)


def solution(mesh):
    return jax.shard_map(
        shards,
        mesh=mesh,
        in_specs=(
            P("member", "grid", None),
            P("member", None, "grid"),
            P(None, "grid"),
            P("grid"),
            P(),
            P(),
            P(),
        ),
        out_specs=(P("member", "grid", None), P("grid", None), P("grid", None)),
        check_vma=False,
    )
```

```python
import functools
import math

import jax
import jax.numpy as jnp
from jax import lax
from jax.experimental import pallas as pl
from jax.experimental.pallas import tpu as pltpu
from jax.sharding import PartitionSpec as P

BF = jnp.bfloat16
F32 = jnp.float32
MEMBERS = 8
V = 100
VS = 112
VP = 128
NCH = 2
BLK = 512
HB = 1024
GB = 4
WB = 512
NWB = 2
ROOT = math.sqrt(2.0 / math.pi)


def dot(a, b):
    return jnp.dot(a, b, preferred_element_type=F32)


def dot_nt(a, b):
    return lax.dot_general(a, b, (((1,), (1,)), ((), ())), preferred_element_type=F32)


def kernel(
    scale,
    hid_hbm, pred_hbm, tgt_hbm, area_hbm, vw_hbm, win_hbm, wout_hbm,
    hgs, win_out, wout_out,
    area, vw, wout_t, hid, win, hT, act, gp, pg, woT,
    psrc, prcv, tgt, gout, gbuf,
    acc, csnd, crcv, oacc, cosnd, corcv, oown,
    s1a, s1b, r1a, r1b, a2, b2,
    s2a, s2b, r2a, r2b, z4, s3, r3, s4, r4,
    lsem, hsem, psem, gsem, csem, x1sem, y1sem, a2sem, b2sem, z3sem, y4sem,
):
    points = hid.shape[0]
    width = hid.shape[1]
    half = points // NCH
    m = lax.axis_index("member")
    g = lax.axis_index("grid")
    y, z_hi = m // 2, m % 2
    x, z_lo, core = g // 8, (g // 2) % 4, g % 2
    z = z_hi * 4 + z_lo

    def dev(xx, yy, zz, cc):
        return (yy * 2 + zz // 4, (xx * 4 + zz % 4) * 2 + cc)

    def member_dev(mm):
        return (mm, g)

    def remote(src, dst, sems, j, target):
        return pltpu.make_async_remote_copy(
            src_ref=src, dst_ref=dst, send_sem=sems.at[0, j], recv_sem=sems.at[1, j],
            device_id=target, device_id_type=pl.DeviceIdType.MESH,
        )

    mine_p = z_hi * 4 + y

    members_far_first = []
    for k, (dy, dz) in enumerate(((2, 1), (1, 1), (3, 1), (0, 1), (2, 0), (1, 0), (3, 0))):
        to_y, to_z = (y + dy) % 4, (z_hi + dz) % 2
        members_far_first.append((1 + k, to_z * 4 + to_y, 2 * to_y + to_z))
    fars = 4

    barrier = pltpu.get_barrier_semaphore()
    partners = [member_dev(to) for _, _, to in members_far_first]
    partners += [dev(x, y, (z + j) % 8, core) for j in (3, 5, 2, 6, 1, 7)]
    partners += [dev((x + j) % 4, y, z, core) for j in (1, 2, 3)]
    partners += [dev(x, y, z, 1 - core)]
    for partner in partners:
        pl.semaphore_signal(barrier, inc=1, device_id=partner, device_id_type=pl.DeviceIdType.MESH)

    win_copy = pltpu.make_async_copy(win_hbm, win, lsem.at[0, 0])
    win_copy.start()
    small_copies = [
        pltpu.make_async_copy(source, target, lsem.at[0, 1 + i])
        for i, (source, target) in enumerate(((area_hbm, area), (vw_hbm, vw), (wout_hbm, wout_t)))
    ]
    for copy in small_copies:
        copy.start()

    def hid_copy(i):
        rows = pl.ds(pl.multiple_of(i * BLK, BLK), BLK)
        return pltpu.make_async_copy(hid_hbm.at[0, rows], hid.at[rows], hsem.at[i])

    own_copies, source_copies = [], []
    for c in range(NCH):
        mine = pl.ds(pl.multiple_of(c * half + 128 * mine_p, 128), 128)
        own_copies.append(pltpu.make_async_copy(pred_hbm.at[0, :, mine], prcv.at[c, mine_p], lsem.at[1, c]))
        own_copies.append(pltpu.make_async_copy(tgt_hbm.at[:, mine], tgt.at[c], lsem.at[2, c]))
        for k in range(MEMBERS):
            cols = pl.ds(c * half + 128 * k, 128)
            source_copies.append(pltpu.make_async_copy(pred_hbm.at[0, :, cols], psrc.at[c, k], lsem.at[3 + k, c]))
    for copy in source_copies + own_copies:
        copy.start()
    hid_copy(0).start()
    for i in range(1, points // BLK):
        hid_copy(i).start()


    def forward(i, carry):
        hid_copy(i).wait()
        rows = pl.ds(pl.multiple_of(i * BLK, BLK), BLK)
        h = hid[rows, :]
        for n in range(0, width, 256):
            u = dot(h, win[:, n:n + 256])
            square = u * u
            t = jnp.tanh(u * (square * (ROOT * 0.044715) + ROOT))
            p = 0.5 * t + 0.5
            a = u * p
            act[rows, n:n + 256] = a.astype(BF)
            gp[rows, n:n + 256] = p + (a * (1.0 - p)) * (square * (ROOT * 0.044715 * 6.0) + 2.0 * ROOT)
        for t8 in range(width // 128):
            turned = jnp.transpose(h[:, t8 * 128:t8 * 128 + 128])
            for q in range(4):
                zl, cc = (t8 % 2) * 2 + q // 2, q % 2
                first = (t8 // 2) * 128 + zl * 32
                hT[cc, first:first + 32, rows] = turned[q * 32:q * 32 + 32, :]
        return carry

    steps = points // BLK

    for copy in source_copies:
        copy.wait()
    pl.semaphore_wait(barrier, len(partners))
    pred_copies = []
    for c in range(NCH):
        chunk = []
        for j, p, to in members_far_first:
            copy = remote(psrc.at[c, p], prcv.at[c, mine_p], psem.at[c], j, member_dev(to))
            copy.start()
            chunk.append(copy)
        pred_copies.append(chunk)

    for copy in small_copies:
        copy.wait()
    gbuf[:, VS:VP, :] = jnp.zeros((NCH * MEMBERS, VP - VS, 128), BF)
    gout[...] = jnp.zeros_like(gout)
    woT[...] = jnp.zeros_like(woT)
    woT[0:V, :] = wout_t[...]
    rows_at = lax.broadcasted_iota(jnp.int32, (V, V), 0)
    cols_at = lax.broadcasted_iota(jnp.int32, (V, V), 1)
    vcol = jnp.sum(jnp.where(rows_at == cols_at, jnp.broadcast_to(vw[...], (V, V)), 0.0), axis=1, keepdims=True)
    win_copy.wait()
    lax.fori_loop(0, steps, forward, 0)

    grad_copies = []
    for c in range(NCH):
        own_copies[2 * c].wait()
        own_copies[2 * c + 1].wait()
        for copy in pred_copies[c]:
            copy.wait_recv()
        cols = pl.ds(pl.multiple_of(c * half + 128 * mine_p, 128), 128)
        weight = vcol * area[:, cols]
        rounded = weight.astype(BF).astype(F32)
        aim = tgt[c].astype(F32)
        preds = [prcv[c, k].astype(F32) for k in range(MEMBERS)]
        counts = [None] * MEMBERS
        for i in range(MEMBERS):
            for k in range(i):
                s = jnp.where(preds[i] > preds[k], 1.0, jnp.where(preds[i] < preds[k], -1.0, 0.0))
                counts[i] = s if counts[i] is None else counts[i] + s
                counts[k] = -s if counts[k] is None else counts[k] - s
        for k in range(MEMBERS):
            s = jnp.where(preds[k] > aim, 1.0, jnp.where(preds[k] < aim, -1.0, 0.0))
            grad = weight * s / MEMBERS - (rounded * counts[k]) / (MEMBERS * (MEMBERS - 1))
            gout[c, k, :V, :] = grad.astype(BF)
        chunk = []
        for j, p, to in members_far_first:
            copy = remote(gout.at[c, p], gbuf.at[c * MEMBERS + mine_p, pl.ds(0, VS)], gsem.at[c], j, member_dev(to))
            copy.start()
            chunk.append(copy)
        gbuf[c * MEMBERS + mine_p, 0:VS, :] = gout[c, mine_p]
        grad_copies.append(chunk)

    def back(i, carry):
        rows = pl.ds(pl.multiple_of(i * (GB * 128), GB * 128), GB * 128)
        turned = jnp.concatenate([jnp.transpose(gbuf[i * GB + k]) for k in range(GB)], axis=0)
        for n in range(0, width, 512):
            pg[rows, n:n + 512] = (dot(turned, woT[:, n:n + 512]) * gp[rows, n:n + 512]).astype(BF)
        return carry

    def hidden_step(i, carry):
        rows = pl.ds(pl.multiple_of(i * HB, HB), HB)
        for n in range(0, width, 256):
            hgs[0, rows, n:n + 256] = dot_nt(pg[rows, :], win[n:n + 256, :]).astype(BF)
        return carry

    other = 1 - core
    sibling = dev(x, y, z, other)
    last = NCH - 1

    group = GB * 128

    def in_tiles(at, which, b):
        rows = pl.ds(*at)
        for n in range(0, WB, 256):
            yield slice(n, n + 256), dot(hT[which, :, rows], pg[rows, b * WB + n:b * WB + n + 256])

    def out_rows(at, first):
        blocks = [gbuf[first + k] for k in range(at[1] // 128)]
        return dot(jnp.concatenate(blocks, axis=1), act[pl.ds(*at), :])

    def add_terms(at, first, start):
        for which in range(2):
            for b in range(NWB):
                for cols, value in in_tiles(at, which, b):
                    acc[which, b, :, cols] = value if start else value + acc[which, b, :, cols]
        oacc[...] = out_rows(at, first) if start else oacc[...] + out_rows(at, first)

    for c in range(last):
        for copy in grad_copies[c]:
            copy.wait_recv()
        for i in range(MEMBERS // GB):
            back(c * (MEMBERS // GB) + i, 0)
        add_terms((c * half, half), c * MEMBERS, c == 0)

    for copy in grad_copies[last][fars:]:
        copy.wait_recv()
    near = last * 2 + z_hi
    back(near, 0)
    add_terms((pl.multiple_of(near * group, group), group), near * GB, False)
    for copy in grad_copies[last][:fars]:
        copy.wait_recv()
    far = last * 2 + 1 - z_hi
    far_at = (pl.multiple_of(far * group, group), group)
    back(far, 0)

    core_copies = []
    for b in range(NWB):
        for cols, value in in_tiles(far_at, other, b):
            csnd[b, :, cols] = (value + acc[other, b, :, cols]).astype(BF)
        copy = remote(csnd.at[b], crcv.at[b], csem, b, sibling)
        copy.start()
        core_copies.append(copy)
    out_term = oacc[...] + out_rows(far_at, far * GB)
    for h8 in range(width // 128):
        turned = jnp.transpose(out_term[:, h8 * 128:h8 * 128 + 128])
        for q in range(4):
            zl, cc = (h8 % 2) * 2 + q // 2, q % 2
            first = (h8 // 2) * 128 + zl * 32
            oown[cc, first:first + 32, :] = turned[q * 32:q * 32 + 32, :]
    cosnd[...] = oown[other].astype(BF)
    copy = remote(cosnd, corcv, csem, NWB, sibling)
    copy.start()
    core_copies.append(copy)

    for b in range(NWB):
        for cols, value in in_tiles(far_at, core, b):
            acc[core, b, :, cols] = value + acc[core, b, :, cols]
        core_copies[b].wait_recv()
        for q in range(4):
            rows = slice(q * 128, q * 128 + 128)
            total = acc[core, b, rows, :] + crcv[b, rows, :].astype(F32)
            acc[core, b, rows, :] = total
            s1a[q, :, b * WB:(b + 1) * WB] = total[0:64, :].astype(BF)
            for yy in range(4):
                s1b[yy, q, :, b * 128:b * 128 + 128] = total[64:128, yy * 128:yy * 128 + 128].astype(BF)
    core_copies[NWB].wait_recv()
    for q in range(4):
        rows = slice(q * 128, q * 128 + 128)
        total = oown[core, rows, :] + corcv[rows, :].astype(F32)
        oown[core, rows, :] = total
        s1a[q, :, width:width + 128] = total[0:64, :].astype(BF)
        s1a[q, :, width + 128:width + 256] = total[64:128, :].astype(BF)
    first = []
    for j in (2, 1, 3):
        xx, yy = (x + j) % 4, (y + j) % 4
        copy = remote(s1a.at[xx], r1a.at[x], x1sem, j, dev(xx, y, z, core))
        copy.start()
        first.append(copy)
        copy = remote(s1b.at[yy], r1b.at[y], y1sem, j, dev(x, yy, z, core))
        copy.start()
        first.append(copy)

    per = points // HB // 2
    lax.fori_loop(0, per, hidden_step, 0)

    own_cols = pl.ds(pl.multiple_of(y * 128, 128), 128)
    own_x = pl.multiple_of(x * 128, 128)
    for copy in first:
        copy.wait_recv()
    for b in range(NWB):
        ta = acc[core, b, pl.ds(own_x, 64), :]
        for j in (1, 2, 3):
            ta = ta + r1a[(x + j) % 4, :, b * WB:(b + 1) * WB].astype(F32)
        a2[b] = ta
        for q in range(4):
            tb = acc[core, b, q * 128 + 64:q * 128 + 128, own_cols]
            for j in (1, 2, 3):
                tb = tb + r1b[(y + j) % 4, q, :, b * 128:b * 128 + 128].astype(F32)
            b2[b, q] = tb
            s2a[q, 64 * b:64 * b + 64, :] = ta[:, q * 128:q * 128 + 128].astype(BF)
            s2b[q, 64 * b:64 * b + 64, :] = tb.astype(BF)
    to = oown[core, pl.ds(own_x, 128), :]
    for j in (1, 2, 3):
        got = r1a[(x + j) % 4, :, width:width + 256].astype(F32)
        to = to + jnp.concatenate([got[:, 0:128], got[:, 128:256]], axis=0)
    for q in range(4):
        part = jnp.concatenate([to[zl * 32 + q * 8:zl * 32 + q * 8 + 8, :] for zl in range(4)], axis=0)
        oown[core, q * 32:q * 32 + 32, :] = part
        s2a[q, 128:160, :] = part.astype(BF)
    second = []
    for j in (1, 2, 3):
        xx, yy = (x + j) % 4, (y + j) % 4
        copy = remote(s2a.at[yy], r2a.at[y], a2sem, j, dev(x, yy, z, core))
        copy.start()
        second.append(copy)
        copy = remote(s2b.at[xx], r2b.at[x], b2sem, j, dev(xx, y, z, core))
        copy.start()
        second.append(copy)
    lax.fori_loop(per, 2 * per, hidden_step, 0)
    for copy in second:
        copy.wait_recv()

    empty = jnp.zeros((8, 128), F32)
    to = oown[core, pl.ds(pl.multiple_of(y * 32, 32), 32), :]
    for j in (1, 2, 3):
        to = to + r2a[(y + j) % 4, 128:160, :].astype(F32)
    sums = []
    for b in range(NWB):
        ta = a2[b, :, own_cols]
        tb = b2[b, x]
        for j in (1, 2, 3):
            ta = ta + r2a[(y + j) % 4, 64 * b:64 * b + 64, :].astype(F32)
            tb = tb + r2b[(x + j) % 4, 64 * b:64 * b + 64, :].astype(F32)
        sums.append((ta[0:32], ta[32:64], tb[0:32], tb[32:64]))
    for q in range(4):
        part = jnp.concatenate([sums[0][q], sums[1][q], to[q * 8:q * 8 + 8, :], empty], axis=0)
        z4[q] = part
        s3[q] = part.astype(BF)
    third = []
    for j in (4, 3, 5, 2, 6, 1, 7):
        zz = (z + j) % 8
        copy = remote(s3.at[zz % 4], r3.at[z], z3sem, j, dev(x, y, zz, core))
        copy.start()
        third.append(copy)
    total = z4[z_lo]
    for copy in third:
        copy.wait_recv()
    for j in range(1, 8):
        total = total + r3[(z + j) % 8].astype(F32)
    total = total * scale
    s4[...] = total.astype(BF)

    fourth = []
    for j in (1, 2, 3):
        copy = remote(s4, r4.at[y], y4sem, j, dev(x, (y + j) % 4, z, core))
        copy.start()
        fourth.append(copy)
    r4[y] = s4[...]
    for chunk in pred_copies + grad_copies:
        for copy in chunk:
            copy.wait_send()
    for copy in core_copies + first + second + third:
        copy.wait_send()
    for copy in fourth:
        copy.wait_recv()
    for q in range(4):
        got = r4[q].astype(F32)
        for b in range(NWB):
            win_out[:, b * WB + q * 128:b * WB + q * 128 + 128] = got[32 * b:32 * b + 32, :]
        wout_out[q * 8:q * 8 + 8, :] = got[64:72, 0:V]
    for copy in fourth:
        copy.wait_send()


def place(hg_in, in_in, out_in, hg_out, in_out, out_out, sem):
    points = hg_in.shape[1]
    parts = 8
    copies = []
    for i in range(parts):
        rows = pl.ds(i * (points // parts), points // parts)
        copies.append(pltpu.make_async_copy(hg_in.at[0, rows], hg_out.at[0, rows], sem.at[i]))
    copies.append(pltpu.make_async_copy(in_in, in_out, sem.at[parts]))
    copies.append(pltpu.make_async_copy(out_in, out_out, sem.at[parts + 1]))
    for copy in copies:
        copy.start()
    for copy in copies:
        copy.wait()


def shards(hidden, pred, target, area, var_weight, w_in, w_out):
    points, width = hidden.shape[1:]
    scale = 1.0 / math.sqrt(points * lax.axis_size("grid") * MEMBERS)
    share = width // lax.axis_size("grid")
    any_spec = pl.BlockSpec(memory_space=pl.ANY)
    vmem_spec = pl.BlockSpec(memory_space=pltpu.VMEM)

    def vm(*shape, dtype=BF):
        return pltpu.VMEM(shape, dtype)

    def sems(*shape):
        return pltpu.SemaphoreType.DMA(shape)

    out_types = (
        jax.ShapeDtypeStruct(hidden.shape, BF),
        jax.ShapeDtypeStruct((share, width), F32),
        jax.ShapeDtypeStruct((share, V), F32),
    )
    half = width // 2
    results = pl.pallas_call(
        functools.partial(kernel, scale),
        out_shape=tuple(pltpu.VMEM(t.shape, t.dtype) for t in out_types),
        in_specs=[any_spec] * 7,
        out_specs=(vmem_spec, vmem_spec, vmem_spec),
        scratch_shapes=[
            vm(1, points, dtype=F32), vm(1, V, dtype=F32), vm(V, width),
            vm(points, width), vm(width, width), vm(2, half, points), vm(points, width),
            vm(points, width, dtype=F32), vm(points, width), vm(VP, width),
            vm(NCH, MEMBERS, V, 128), vm(NCH, MEMBERS, V, 128), vm(NCH, V, 128), vm(NCH, MEMBERS, VS, 128),
            vm(NCH * MEMBERS, VP, 128),
            vm(2, NWB, half, WB, dtype=F32), vm(NWB, half, WB), vm(NWB, half, WB),
            vm(VP, width, dtype=F32), vm(half, VP), vm(half, VP), vm(2, half, VP, dtype=F32),
            vm(4, 64, width + 256), vm(4, 4, 64, 256), vm(4, 64, width + 256), vm(4, 4, 64, 256),
            vm(NWB, 64, WB, dtype=F32), vm(NWB, 4, 64, 128, dtype=F32),
            vm(4, 160, 128), vm(4, 128, 128), vm(4, 160, 128), vm(4, 128, 128),
            vm(4, 80, 128, dtype=F32), vm(4, 80, 128), vm(8, 80, 128), vm(80, 128), vm(4, 80, 128),
            sems(3 + MEMBERS, 4), sems(points // BLK),
            sems(NCH, 2, MEMBERS), sems(NCH, 2, MEMBERS), sems(2, NWB + 1),
            sems(2, 4), sems(2, 4), sems(2, 4), sems(2, 4), sems(2, 8), sems(2, 4),
        ],
        compiler_params=pltpu.CompilerParams(
            collective_id=0, has_side_effects=True, vmem_limit_bytes=50 * 1024 * 1024
        ),
    )(hidden, pred, target, area.reshape(1, -1), var_weight.reshape(1, -1), w_in, w_out.T)
    return pl.pallas_call(
        place,
        out_shape=out_types,
        in_specs=[vmem_spec] * 3,
        out_specs=(any_spec,) * 3,
        scratch_shapes=[sems(10)],
        compiler_params=pltpu.CompilerParams(vmem_limit_bytes=8 * 1024 * 1024),
    )(*results)


def solution(mesh):
    return jax.shard_map(
        shards,
        mesh=mesh,
        in_specs=(
            P("member", "grid", None),
            P("member", None, "grid"),
            P(None, "grid"),
            P("grid"),
            P(),
            P(),
            P(),
        ),
        out_specs=(P("member", "grid", None), P("grid", None), P("grid", None)),
        check_vma=False,
    )
```

```python
import functools
import math

import jax
import jax.numpy as jnp
from jax import lax
from jax.experimental import pallas as pl
from jax.experimental.pallas import tpu as pltpu
from jax.sharding import PartitionSpec as P

BF = jnp.bfloat16
F32 = jnp.float32
MEMBERS = 8
V = 100
VS = 112
VP = 128
NCH = 1
BLK = 512
HB = 1024
GB = 4
WB = 512
NWB = 2
ROOT = math.sqrt(2.0 / math.pi)


def dot(a, b):
    return jnp.dot(a, b, preferred_element_type=F32)


def dot_nt(a, b):
    return lax.dot_general(a, b, (((1,), (1,)), ((), ())), preferred_element_type=F32)


def kernel(
    scale,
    hid_hbm, pred_hbm, tgt_hbm, area_hbm, vw_hbm, win_hbm, wout_hbm,
    hgs, win_out, wout_out,
    area, vw, wout_t, hid, win, hT, act, gp, pg, woT,
    psrc, prcv, tgt, gout, gbuf,
    acc, csnd, crcv, oacc, cosnd, corcv, oown,
    s1a, s1b, r1a, r1b, a2, b2,
    s2a, s2b, r2a, r2b, z4, s3, r3, s4, r4,
    lsem, hsem, psem, gsem, csem, x1sem, y1sem, a2sem, b2sem, z3sem, y4sem,
):
    points = hid.shape[0]
    width = hid.shape[1]
    half = points // NCH
    pb = half // MEMBERS
    m = lax.axis_index("member")
    g = lax.axis_index("grid")
    y, z_hi = m // 2, m % 2
    x, z_lo, core = g // 8, (g // 2) % 4, g % 2
    z = z_hi * 4 + z_lo

    def dev(xx, yy, zz, cc):
        return (yy * 2 + zz // 4, (xx * 4 + zz % 4) * 2 + cc)

    def member_dev(mm):
        return (mm, g)

    def remote(src, dst, sems, j, target):
        return pltpu.make_async_remote_copy(
            src_ref=src, dst_ref=dst, send_sem=sems.at[0, j], recv_sem=sems.at[1, j],
            device_id=target, device_id_type=pl.DeviceIdType.MESH,
        )

    mine_p = z_hi * 4 + y

    members_far_first = []
    for k, (dy, dz) in enumerate(((2, 1), (1, 1), (3, 1), (0, 1), (2, 0), (1, 0), (3, 0))):
        to_y, to_z = (y + dy) % 4, (z_hi + dz) % 2
        members_far_first.append((1 + k, to_z * 4 + to_y, 2 * to_y + to_z))
    fars = 4

    barrier = pltpu.get_barrier_semaphore()
    partners = [member_dev(to) for _, _, to in members_far_first]
    partners += [dev(x, y, (z + j) % 8, core) for j in (3, 5, 2, 6, 1, 7)]
    partners += [dev((x + j) % 4, y, z, core) for j in (1, 2, 3)]
    partners += [dev(x, y, z, 1 - core)]
    for partner in partners:
        pl.semaphore_signal(barrier, inc=1, device_id=partner, device_id_type=pl.DeviceIdType.MESH)

    win_copy = pltpu.make_async_copy(win_hbm, win, lsem.at[0, 0])
    win_copy.start()
    small_copies = [
        pltpu.make_async_copy(source, target, lsem.at[0, 1 + i])
        for i, (source, target) in enumerate(((area_hbm, area), (vw_hbm, vw), (wout_hbm, wout_t)))
    ]
    for copy in small_copies:
        copy.start()

    def hid_copy(i):
        rows = pl.ds(pl.multiple_of(i * BLK, BLK), BLK)
        return pltpu.make_async_copy(hid_hbm.at[0, rows], hid.at[rows], hsem.at[i])

    own_copies, source_copies = [], []
    for c in range(NCH):
        mine = pl.ds(pl.multiple_of(c * half + pb * mine_p, pb), pb)
        own_copies.append(pltpu.make_async_copy(pred_hbm.at[0, :, mine], prcv.at[c, mine_p], lsem.at[1, c]))
        own_copies.append(pltpu.make_async_copy(tgt_hbm.at[:, mine], tgt.at[c], lsem.at[2, c]))
        for k in range(MEMBERS):
            cols = pl.ds(c * half + pb * k, pb)
            source_copies.append(pltpu.make_async_copy(pred_hbm.at[0, :, cols], psrc.at[c, k], lsem.at[3 + k, c]))
    for copy in source_copies + own_copies:
        copy.start()
    hid_copy(0).start()
    for i in range(1, points // BLK):
        hid_copy(i).start()


    def forward(i, carry):
        hid_copy(i).wait()
        rows = pl.ds(pl.multiple_of(i * BLK, BLK), BLK)
        h = hid[rows, :]
        for n in range(0, width, 256):
            u = dot(h, win[:, n:n + 256])
            square = u * u
            t = jnp.tanh(u * (square * (ROOT * 0.044715) + ROOT))
            p = 0.5 * t + 0.5
            a = u * p
            act[rows, n:n + 256] = a.astype(BF)
            gp[rows, n:n + 256] = p + (a * (1.0 - p)) * (square * (ROOT * 0.044715 * 6.0) + 2.0 * ROOT)
        for t8 in range(width // 128):
            turned = jnp.transpose(h[:, t8 * 128:t8 * 128 + 128])
            for q in range(4):
                zl, cc = (t8 % 2) * 2 + q // 2, q % 2
                first = (t8 // 2) * 128 + zl * 32
                hT[cc, first:first + 32, rows] = turned[q * 32:q * 32 + 32, :]
        return carry

    steps = points // BLK

    for copy in source_copies:
        copy.wait()
    pl.semaphore_wait(barrier, len(partners))
    pred_copies = []
    for c in range(NCH):
        chunk = []
        for j, p, to in members_far_first:
            copy = remote(psrc.at[c, p], prcv.at[c, mine_p], psem.at[c], j, member_dev(to))
            copy.start()
            chunk.append(copy)
        pred_copies.append(chunk)

    for copy in small_copies:
        copy.wait()
    gbuf[:, VS:VP, :] = jnp.zeros((NCH * MEMBERS, VP - VS, pb), BF)
    gout[...] = jnp.zeros_like(gout)
    woT[...] = jnp.zeros_like(woT)
    woT[0:V, :] = wout_t[...]
    rows_at = lax.broadcasted_iota(jnp.int32, (V, V), 0)
    cols_at = lax.broadcasted_iota(jnp.int32, (V, V), 1)
    vcol = jnp.sum(jnp.where(rows_at == cols_at, jnp.broadcast_to(vw[...], (V, V)), 0.0), axis=1, keepdims=True)
    win_copy.wait()
    lax.fori_loop(0, steps, forward, 0)

    grad_copies = []
    for c in range(NCH):
        own_copies[2 * c].wait()
        own_copies[2 * c + 1].wait()
        for copy in pred_copies[c]:
            copy.wait_recv()
        cols = pl.ds(pl.multiple_of(c * half + pb * mine_p, pb), pb)
        weight = vcol * area[:, cols]
        rounded = weight.astype(BF).astype(F32)
        aim = tgt[c].astype(F32)
        preds = [prcv[c, k].astype(F32) for k in range(MEMBERS)]
        counts = [None] * MEMBERS
        for i in range(MEMBERS):
            for k in range(i):
                s = jnp.where(preds[i] > preds[k], 1.0, jnp.where(preds[i] < preds[k], -1.0, 0.0))
                counts[i] = s if counts[i] is None else counts[i] + s
                counts[k] = -s if counts[k] is None else counts[k] - s
        for k in range(MEMBERS):
            s = jnp.where(preds[k] > aim, 1.0, jnp.where(preds[k] < aim, -1.0, 0.0))
            grad = weight * s / MEMBERS - (rounded * counts[k]) / (MEMBERS * (MEMBERS - 1))
            gout[c, k, :V, :] = grad.astype(BF)
        chunk = []
        for j, p, to in members_far_first:
            copy = remote(gout.at[c, p], gbuf.at[c * MEMBERS + mine_p, pl.ds(0, VS)], gsem.at[c], j, member_dev(to))
            copy.start()
            chunk.append(copy)
        gbuf[c * MEMBERS + mine_p, 0:VS, :] = gout[c, mine_p]
        grad_copies.append(chunk)

    def back(i, carry):
        rows = pl.ds(pl.multiple_of(i * (GB * pb), GB * pb), GB * pb)
        turned = jnp.concatenate([jnp.transpose(gbuf[i * GB + k]) for k in range(GB)], axis=0)
        for n in range(0, width, 512):
            pg[rows, n:n + 512] = (dot(turned, woT[:, n:n + 512]) * gp[rows, n:n + 512]).astype(BF)
        return carry

    def hidden_step(i, carry):
        rows = pl.ds(pl.multiple_of(i * HB, HB), HB)
        for n in range(0, width, 256):
            hgs[0, rows, n:n + 256] = dot_nt(pg[rows, :], win[n:n + 256, :]).astype(BF)
        return carry

    other = 1 - core
    sibling = dev(x, y, z, other)
    last = NCH - 1

    group = GB * pb

    def in_tiles(at, which, b):
        rows = pl.ds(*at)
        for n in range(0, WB, 256):
            yield slice(n, n + 256), dot(hT[which, :, rows], pg[rows, b * WB + n:b * WB + n + 256])

    def out_rows(at, first):
        blocks = [gbuf[first + k] for k in range(at[1] // pb)]
        return dot(jnp.concatenate(blocks, axis=1), act[pl.ds(*at), :])

    def add_terms(at, first, start):
        for which in range(2):
            for b in range(NWB):
                for cols, value in in_tiles(at, which, b):
                    acc[which, b, :, cols] = value if start else value + acc[which, b, :, cols]
        oacc[...] = out_rows(at, first) if start else oacc[...] + out_rows(at, first)

    for c in range(last):
        for copy in grad_copies[c]:
            copy.wait_recv()
        for i in range(MEMBERS // GB):
            back(c * (MEMBERS // GB) + i, 0)
        add_terms((c * half, half), c * MEMBERS, c == 0)

    for copy in grad_copies[last][fars:]:
        copy.wait_recv()
    near = last * 2 + z_hi
    back(near, 0)
    add_terms((pl.multiple_of(near * group, group), group), near * GB, last == 0)
    for copy in grad_copies[last][:fars]:
        copy.wait_recv()
    far = last * 2 + 1 - z_hi
    far_at = (pl.multiple_of(far * group, group), group)
    back(far, 0)

    core_copies = []
    for b in range(NWB):
        for cols, value in in_tiles(far_at, other, b):
            csnd[b, :, cols] = (value + acc[other, b, :, cols]).astype(BF)
        copy = remote(csnd.at[b], crcv.at[b], csem, b, sibling)
        copy.start()
        core_copies.append(copy)
    out_term = oacc[...] + out_rows(far_at, far * GB)
    for h8 in range(width // 128):
        turned = jnp.transpose(out_term[:, h8 * 128:h8 * 128 + 128])
        for q in range(4):
            zl, cc = (h8 % 2) * 2 + q // 2, q % 2
            first = (h8 // 2) * 128 + zl * 32
            oown[cc, first:first + 32, :] = turned[q * 32:q * 32 + 32, :]
    cosnd[...] = oown[other].astype(BF)
    copy = remote(cosnd, corcv, csem, NWB, sibling)
    copy.start()
    core_copies.append(copy)

    for b in range(NWB):
        for cols, value in in_tiles(far_at, core, b):
            acc[core, b, :, cols] = value + acc[core, b, :, cols]
        core_copies[b].wait_recv()
        for q in range(4):
            rows = slice(q * 128, q * 128 + 128)
            total = acc[core, b, rows, :] + crcv[b, rows, :].astype(F32)
            acc[core, b, rows, :] = total
            s1a[q, :, b * WB:(b + 1) * WB] = total[0:64, :].astype(BF)
            for yy in range(4):
                s1b[yy, q, :, b * 128:b * 128 + 128] = total[64:128, yy * 128:yy * 128 + 128].astype(BF)
    core_copies[NWB].wait_recv()
    for q in range(4):
        rows = slice(q * 128, q * 128 + 128)
        total = oown[core, rows, :] + corcv[rows, :].astype(F32)
        oown[core, rows, :] = total
        s1a[q, :, width:width + 128] = total[0:64, :].astype(BF)
        s1a[q, :, width + 128:width + 256] = total[64:128, :].astype(BF)
    first = []
    for j in (2, 1, 3):
        xx, yy = (x + j) % 4, (y + j) % 4
        copy = remote(s1a.at[xx], r1a.at[x], x1sem, j, dev(xx, y, z, core))
        copy.start()
        first.append(copy)
        copy = remote(s1b.at[yy], r1b.at[y], y1sem, j, dev(x, yy, z, core))
        copy.start()
        first.append(copy)

    per = points // HB // 2
    lax.fori_loop(0, per, hidden_step, 0)

    own_cols = pl.ds(pl.multiple_of(y * 128, 128), 128)
    own_x = pl.multiple_of(x * 128, 128)
    for copy in first:
        copy.wait_recv()
    for b in range(NWB):
        ta = acc[core, b, pl.ds(own_x, 64), :]
        for j in (1, 2, 3):
            ta = ta + r1a[(x + j) % 4, :, b * WB:(b + 1) * WB].astype(F32)
        a2[b] = ta
        for q in range(4):
            tb = acc[core, b, q * 128 + 64:q * 128 + 128, own_cols]
            for j in (1, 2, 3):
                tb = tb + r1b[(y + j) % 4, q, :, b * 128:b * 128 + 128].astype(F32)
            b2[b, q] = tb
            s2a[q, 64 * b:64 * b + 64, :] = ta[:, q * 128:q * 128 + 128].astype(BF)
            s2b[q, 64 * b:64 * b + 64, :] = tb.astype(BF)
    to = oown[core, pl.ds(own_x, 128), :]
    for j in (1, 2, 3):
        got = r1a[(x + j) % 4, :, width:width + 256].astype(F32)
        to = to + jnp.concatenate([got[:, 0:128], got[:, 128:256]], axis=0)
    for q in range(4):
        part = jnp.concatenate([to[zl * 32 + q * 8:zl * 32 + q * 8 + 8, :] for zl in range(4)], axis=0)
        oown[core, q * 32:q * 32 + 32, :] = part
        s2a[q, 128:160, :] = part.astype(BF)
    second = []
    for j in (1, 2, 3):
        xx, yy = (x + j) % 4, (y + j) % 4
        copy = remote(s2a.at[yy], r2a.at[y], a2sem, j, dev(x, yy, z, core))
        copy.start()
        second.append(copy)
        copy = remote(s2b.at[xx], r2b.at[x], b2sem, j, dev(xx, y, z, core))
        copy.start()
        second.append(copy)
    lax.fori_loop(per, 2 * per, hidden_step, 0)
    for copy in second:
        copy.wait_recv()

    empty = jnp.zeros((8, 128), F32)
    to = oown[core, pl.ds(pl.multiple_of(y * 32, 32), 32), :]
    for j in (1, 2, 3):
        to = to + r2a[(y + j) % 4, 128:160, :].astype(F32)
    sums = []
    for b in range(NWB):
        ta = a2[b, :, own_cols]
        tb = b2[b, x]
        for j in (1, 2, 3):
            ta = ta + r2a[(y + j) % 4, 64 * b:64 * b + 64, :].astype(F32)
            tb = tb + r2b[(x + j) % 4, 64 * b:64 * b + 64, :].astype(F32)
        sums.append((ta[0:32], ta[32:64], tb[0:32], tb[32:64]))
    for q in range(4):
        part = jnp.concatenate([sums[0][q], sums[1][q], to[q * 8:q * 8 + 8, :], empty], axis=0)
        z4[q] = part
        s3[q] = part.astype(BF)
    third = []
    for j in (4, 3, 5, 2, 6, 1, 7):
        zz = (z + j) % 8
        copy = remote(s3.at[zz % 4], r3.at[z], z3sem, j, dev(x, y, zz, core))
        copy.start()
        third.append(copy)
    total = z4[z_lo]
    for copy in third:
        copy.wait_recv()
    for j in range(1, 8):
        total = total + r3[(z + j) % 8].astype(F32)
    total = total * scale
    s4[...] = total.astype(BF)

    fourth = []
    for j in (1, 2, 3):
        copy = remote(s4, r4.at[y], y4sem, j, dev(x, (y + j) % 4, z, core))
        copy.start()
        fourth.append(copy)
    r4[y] = s4[...]
    for chunk in pred_copies + grad_copies:
        for copy in chunk:
            copy.wait_send()
    for copy in core_copies + first + second + third:
        copy.wait_send()
    for copy in fourth:
        copy.wait_recv()
    for q in range(4):
        got = r4[q].astype(F32)
        for b in range(NWB):
            win_out[:, b * WB + q * 128:b * WB + q * 128 + 128] = got[32 * b:32 * b + 32, :]
        wout_out[q * 8:q * 8 + 8, :] = got[64:72, 0:V]
    for copy in fourth:
        copy.wait_send()


def place(hg_in, in_in, out_in, hg_out, in_out, out_out, sem):
    points = hg_in.shape[1]
    parts = 8
    copies = []
    for i in range(parts):
        rows = pl.ds(i * (points // parts), points // parts)
        copies.append(pltpu.make_async_copy(hg_in.at[0, rows], hg_out.at[0, rows], sem.at[i]))
    copies.append(pltpu.make_async_copy(in_in, in_out, sem.at[parts]))
    copies.append(pltpu.make_async_copy(out_in, out_out, sem.at[parts + 1]))
    for copy in copies:
        copy.start()
    for copy in copies:
        copy.wait()


def shards(hidden, pred, target, area, var_weight, w_in, w_out):
    points, width = hidden.shape[1:]
    scale = 1.0 / math.sqrt(points * lax.axis_size("grid") * MEMBERS)
    share = width // lax.axis_size("grid")
    any_spec = pl.BlockSpec(memory_space=pl.ANY)
    vmem_spec = pl.BlockSpec(memory_space=pltpu.VMEM)

    def vm(*shape, dtype=BF):
        return pltpu.VMEM(shape, dtype)

    def sems(*shape):
        return pltpu.SemaphoreType.DMA(shape)

    out_types = (
        jax.ShapeDtypeStruct(hidden.shape, BF),
        jax.ShapeDtypeStruct((share, width), F32),
        jax.ShapeDtypeStruct((share, V), F32),
    )
    half = width // 2
    pb = points // (NCH * MEMBERS)
    results = pl.pallas_call(
        functools.partial(kernel, scale),
        out_shape=tuple(pltpu.VMEM(t.shape, t.dtype) for t in out_types),
        in_specs=[any_spec] * 7,
        out_specs=(vmem_spec, vmem_spec, vmem_spec),
        scratch_shapes=[
            vm(1, points, dtype=F32), vm(1, V, dtype=F32), vm(V, width),
            vm(points, width), vm(width, width), vm(2, half, points), vm(points, width),
            vm(points, width, dtype=F32), vm(points, width), vm(VP, width),
            vm(NCH, MEMBERS, V, pb), vm(NCH, MEMBERS, V, pb), vm(NCH, V, pb), vm(NCH, MEMBERS, VS, pb),
            vm(NCH * MEMBERS, VP, pb),
            vm(2, NWB, half, WB, dtype=F32), vm(NWB, half, WB), vm(NWB, half, WB),
            vm(VP, width, dtype=F32), vm(half, VP), vm(half, VP), vm(2, half, VP, dtype=F32),
            vm(4, 64, width + 256), vm(4, 4, 64, 256), vm(4, 64, width + 256), vm(4, 4, 64, 256),
            vm(NWB, 64, WB, dtype=F32), vm(NWB, 4, 64, 128, dtype=F32),
            vm(4, 160, 128), vm(4, 128, 128), vm(4, 160, 128), vm(4, 128, 128),
            vm(4, 80, 128, dtype=F32), vm(4, 80, 128), vm(8, 80, 128), vm(80, 128), vm(4, 80, 128),
            sems(3 + MEMBERS, 4), sems(points // BLK),
            sems(NCH, 2, MEMBERS), sems(NCH, 2, MEMBERS), sems(2, NWB + 1),
            sems(2, 4), sems(2, 4), sems(2, 4), sems(2, 4), sems(2, 8), sems(2, 4),
        ],
        compiler_params=pltpu.CompilerParams(
            collective_id=0, has_side_effects=True, vmem_limit_bytes=50 * 1024 * 1024
        ),
    )(hidden, pred, target, area.reshape(1, -1), var_weight.reshape(1, -1), w_in, w_out.T)
    return pl.pallas_call(
        place,
        out_shape=out_types,
        in_specs=[vmem_spec] * 3,
        out_specs=(any_spec,) * 3,
        scratch_shapes=[sems(10)],
        compiler_params=pltpu.CompilerParams(vmem_limit_bytes=8 * 1024 * 1024),
    )(*results)


def solution(mesh):
    return jax.shard_map(
        shards,
        mesh=mesh,
        in_specs=(
            P("member", "grid", None),
            P("member", None, "grid"),
            P(None, "grid"),
            P("grid"),
            P(),
            P(),
            P(),
        ),
        out_specs=(P("member", "grid", None), P("grid", None), P("grid", None)),
        check_vma=False,
    )
```

```python
import functools
import math

import jax
import jax.numpy as jnp
from jax import lax
from jax.experimental import pallas as pl
from jax.experimental.pallas import tpu as pltpu
from jax.sharding import PartitionSpec as P

BF = jnp.bfloat16
F32 = jnp.float32
MEMBERS = 8
V = 100
VS = 112
VP = 128
NCH = 1
BLK = 512
HB = 1024
GB = 4
WB = 512
NWB = 2
ROOT = math.sqrt(2.0 / math.pi)


def dot(a, b):
    return jnp.dot(a, b, preferred_element_type=F32)


def dot_nt(a, b):
    return lax.dot_general(a, b, (((1,), (1,)), ((), ())), preferred_element_type=F32)


def kernel(
    scale,
    hid_hbm, pred_hbm, tgt_hbm, area_hbm, vw_hbm, win_hbm, wout_hbm,
    hgs, win_out, wout_out,
    area, vw, wout_t, hid, win, hT, act, gp, pg, woT,
    psrc, prcv, tgt, gout, gbuf,
    acc, csnd, crcv, oacc, cosnd, corcv, oown,
    s1a, s1b, r1a, r1b, a2, b2,
    s2a, s2b, r2a, r2b, z4, s3, r3, s4, r4,
    lsem, hsem, psem, gsem, csem, x1sem, y1sem, a2sem, b2sem, z3sem, y4sem,
):
    points = hid.shape[0]
    width = hid.shape[1]
    half = points // NCH
    pb = half // MEMBERS
    m = lax.axis_index("member")
    g = lax.axis_index("grid")
    y, z_hi = m // 2, m % 2
    x, z_lo, core = g // 8, (g // 2) % 4, g % 2
    z = z_hi * 4 + z_lo

    def dev(xx, yy, zz, cc):
        return (yy * 2 + zz // 4, (xx * 4 + zz % 4) * 2 + cc)

    def member_dev(mm):
        return (mm, g)

    def remote(src, dst, sems, j, target):
        return pltpu.make_async_remote_copy(
            src_ref=src, dst_ref=dst, send_sem=sems.at[0, j], recv_sem=sems.at[1, j],
            device_id=target, device_id_type=pl.DeviceIdType.MESH,
        )

    mine_p = z_hi * 4 + y

    members_far_first = []
    for k, (dy, dz) in enumerate(((2, 1), (1, 1), (3, 1), (0, 1), (2, 0), (1, 0), (3, 0))):
        to_y, to_z = (y + dy) % 4, (z_hi + dz) % 2
        members_far_first.append((1 + k, to_z * 4 + to_y, 2 * to_y + to_z))
    fars = 4

    barrier = pltpu.get_barrier_semaphore()
    partners = [member_dev(to) for _, _, to in members_far_first]
    partners += [dev(x, y, (z + j) % 8, core) for j in (3, 5, 2, 6, 1, 7)]
    partners += [dev((x + j) % 4, y, z, core) for j in (1, 2, 3)]
    partners += [dev(x, y, z, 1 - core)]
    for partner in partners:
        pl.semaphore_signal(barrier, inc=1, device_id=partner, device_id_type=pl.DeviceIdType.MESH)

    win_copy = pltpu.make_async_copy(win_hbm, win, lsem.at[0, 0])
    win_copy.start()
    small_copies = [
        pltpu.make_async_copy(source, target, lsem.at[0, 1 + i])
        for i, (source, target) in enumerate(((area_hbm, area), (vw_hbm, vw), (wout_hbm, wout_t)))
    ]
    for copy in small_copies:
        copy.start()

    def hid_copy(i):
        rows = pl.ds(pl.multiple_of(i * BLK, BLK), BLK)
        return pltpu.make_async_copy(hid_hbm.at[0, rows], hid.at[rows], hsem.at[i])

    own_copies, source_copies = [], []
    for c in range(NCH):
        mine = pl.ds(pl.multiple_of(c * half + pb * mine_p, pb), pb)
        own_copies.append(pltpu.make_async_copy(pred_hbm.at[0, :, mine], prcv.at[c, mine_p], lsem.at[1, c]))
        own_copies.append(pltpu.make_async_copy(tgt_hbm.at[:, mine], tgt.at[c], lsem.at[2, c]))
        for k in range(MEMBERS):
            cols = pl.ds(c * half + pb * k, pb)
            source_copies.append(pltpu.make_async_copy(pred_hbm.at[0, :, cols], psrc.at[c, k], lsem.at[3 + k, c]))
    for copy in source_copies + own_copies:
        copy.start()
    hid_copy(0).start()
    for i in range(1, points // BLK):
        hid_copy(i).start()


    def forward(i, carry):
        hid_copy(i).wait()
        rows = pl.ds(pl.multiple_of(i * BLK, BLK), BLK)
        h = hid[rows, :]
        for n in range(0, width, 256):
            u = dot(h, win[:, n:n + 256])
            square = u * u
            t = jnp.tanh(u * (square * (ROOT * 0.044715) + ROOT))
            p = 0.5 * t + 0.5
            a = u * p
            act[rows, n:n + 256] = a.astype(BF)
            gp[rows, n:n + 256] = p + (a * (1.0 - p)) * (square * (ROOT * 0.044715 * 6.0) + 2.0 * ROOT)
        for t8 in range(width // 128):
            turned = jnp.transpose(h[:, t8 * 128:t8 * 128 + 128])
            for q in range(4):
                zl, cc = (t8 % 2) * 2 + q // 2, q % 2
                first = (t8 // 2) * 128 + zl * 32
                hT[cc, first:first + 32, rows] = turned[q * 32:q * 32 + 32, :]
        return carry

    steps = points // BLK

    for copy in source_copies:
        copy.wait()
    pl.semaphore_wait(barrier, len(partners))
    pred_copies = []
    for c in range(NCH):
        chunk = []
        for j, p, to in members_far_first:
            copy = remote(psrc.at[c, p], prcv.at[c, mine_p], psem.at[c], j, member_dev(to))
            copy.start()
            chunk.append(copy)
        pred_copies.append(chunk)

    for copy in small_copies:
        copy.wait()
    gbuf[:, VS:VP, :] = jnp.zeros((NCH * MEMBERS, VP - VS, pb), BF)
    gout[...] = jnp.zeros_like(gout)
    woT[...] = jnp.zeros_like(woT)
    woT[0:V, :] = wout_t[...]
    rows_at = lax.broadcasted_iota(jnp.int32, (V, V), 0)
    cols_at = lax.broadcasted_iota(jnp.int32, (V, V), 1)
    vcol = jnp.sum(jnp.where(rows_at == cols_at, jnp.broadcast_to(vw[...], (V, V)), 0.0), axis=1, keepdims=True)
    win_copy.wait()
    lax.fori_loop(0, steps, forward, 0)

    grad_copies = []
    for c in range(NCH):
        own_copies[2 * c].wait()
        own_copies[2 * c + 1].wait()
        for copy in pred_copies[c]:
            copy.wait_recv()
        cols = pl.ds(pl.multiple_of(c * half + pb * mine_p, pb), pb)
        weight = vcol * area[:, cols]
        rounded = weight.astype(BF).astype(F32)
        aim = tgt[c].astype(F32)
        preds = [prcv[c, k].astype(F32) for k in range(MEMBERS)]
        counts = [None] * MEMBERS
        for i in range(MEMBERS):
            for k in range(i):
                s = jnp.where(preds[i] > preds[k], 1.0, jnp.where(preds[i] < preds[k], -1.0, 0.0))
                counts[i] = s if counts[i] is None else counts[i] + s
                counts[k] = -s if counts[k] is None else counts[k] - s
        for k in range(MEMBERS):
            s = jnp.where(preds[k] > aim, 1.0, jnp.where(preds[k] < aim, -1.0, 0.0))
            grad = weight * s / MEMBERS - (rounded * counts[k]) / (MEMBERS * (MEMBERS - 1))
            gout[c, k, :V, :] = grad.astype(BF)
        chunk = []
        for j, p, to in members_far_first[fars:] + members_far_first[:fars]:
            copy = remote(gout.at[c, p], gbuf.at[c * MEMBERS + mine_p, pl.ds(0, VS)], gsem.at[c], j, member_dev(to))
            copy.start()
            chunk.append(copy)
        gbuf[c * MEMBERS + mine_p, 0:VS, :] = gout[c, mine_p]
        grad_copies.append(chunk)

    def back(i, carry):
        rows = pl.ds(pl.multiple_of(i * (GB * pb), GB * pb), GB * pb)
        turned = jnp.concatenate([jnp.transpose(gbuf[i * GB + k]) for k in range(GB)], axis=0)
        for n in range(0, width, 512):
            pg[rows, n:n + 512] = (dot(turned, woT[:, n:n + 512]) * gp[rows, n:n + 512]).astype(BF)
        return carry

    def hidden_step(i, carry):
        rows = pl.ds(pl.multiple_of(i * HB, HB), HB)
        for n in range(0, width, 256):
            hgs[0, rows, n:n + 256] = dot_nt(pg[rows, :], win[n:n + 256, :]).astype(BF)
        return carry

    other = 1 - core
    sibling = dev(x, y, z, other)
    last = NCH - 1

    group = GB * pb

    def in_tiles(at, which, b):
        rows = pl.ds(*at)
        for n in range(0, WB, 256):
            yield slice(n, n + 256), dot(hT[which, :, rows], pg[rows, b * WB + n:b * WB + n + 256])

    def out_rows(at, first):
        blocks = [gbuf[first + k] for k in range(at[1] // pb)]
        return dot(jnp.concatenate(blocks, axis=1), act[pl.ds(*at), :])

    def add_terms(at, first, start):
        for which in range(2):
            for b in range(NWB):
                for cols, value in in_tiles(at, which, b):
                    acc[which, b, :, cols] = value if start else value + acc[which, b, :, cols]
        oacc[...] = out_rows(at, first) if start else oacc[...] + out_rows(at, first)

    for c in range(last):
        for copy in grad_copies[c]:
            copy.wait_recv()
        for i in range(MEMBERS // GB):
            back(c * (MEMBERS // GB) + i, 0)
        add_terms((c * half, half), c * MEMBERS, c == 0)

    for copy in grad_copies[last][:MEMBERS - 1 - fars]:
        copy.wait_recv()
    near = last * 2 + z_hi
    back(near, 0)
    add_terms((pl.multiple_of(near * group, group), group), near * GB, last == 0)
    for copy in grad_copies[last][MEMBERS - 1 - fars:]:
        copy.wait_recv()
    far = last * 2 + 1 - z_hi
    far_at = (pl.multiple_of(far * group, group), group)
    back(far, 0)

    core_copies = []
    for b in range(NWB):
        for cols, value in in_tiles(far_at, other, b):
            csnd[b, :, cols] = (value + acc[other, b, :, cols]).astype(BF)
        copy = remote(csnd.at[b], crcv.at[b], csem, b, sibling)
        copy.start()
        core_copies.append(copy)
    out_term = oacc[...] + out_rows(far_at, far * GB)
    for h8 in range(width // 128):
        turned = jnp.transpose(out_term[:, h8 * 128:h8 * 128 + 128])
        for q in range(4):
            zl, cc = (h8 % 2) * 2 + q // 2, q % 2
            first = (h8 // 2) * 128 + zl * 32
            oown[cc, first:first + 32, :] = turned[q * 32:q * 32 + 32, :]
    cosnd[...] = oown[other].astype(BF)
    copy = remote(cosnd, corcv, csem, NWB, sibling)
    copy.start()
    core_copies.append(copy)

    for b in range(NWB):
        for cols, value in in_tiles(far_at, core, b):
            acc[core, b, :, cols] = value + acc[core, b, :, cols]
        core_copies[b].wait_recv()
        for q in range(4):
            rows = slice(q * 128, q * 128 + 128)
            total = acc[core, b, rows, :] + crcv[b, rows, :].astype(F32)
            acc[core, b, rows, :] = total
            s1a[q, :, b * WB:(b + 1) * WB] = total[0:64, :].astype(BF)
            for yy in range(4):
                s1b[yy, q, :, b * 128:b * 128 + 128] = total[64:128, yy * 128:yy * 128 + 128].astype(BF)
    core_copies[NWB].wait_recv()
    for q in range(4):
        rows = slice(q * 128, q * 128 + 128)
        total = oown[core, rows, :] + corcv[rows, :].astype(F32)
        oown[core, rows, :] = total
        s1a[q, :, width:width + 128] = total[0:64, :].astype(BF)
        s1a[q, :, width + 128:width + 256] = total[64:128, :].astype(BF)
    first = []
    for j in (2, 1, 3):
        xx, yy = (x + j) % 4, (y + j) % 4
        copy = remote(s1a.at[xx], r1a.at[x], x1sem, j, dev(xx, y, z, core))
        copy.start()
        first.append(copy)
        copy = remote(s1b.at[yy], r1b.at[y], y1sem, j, dev(x, yy, z, core))
        copy.start()
        first.append(copy)

    per = points // HB // 2
    lax.fori_loop(0, per, hidden_step, 0)

    own_cols = pl.ds(pl.multiple_of(y * 128, 128), 128)
    own_x = pl.multiple_of(x * 128, 128)
    for copy in first:
        copy.wait_recv()
    for b in range(NWB):
        ta = acc[core, b, pl.ds(own_x, 64), :]
        for j in (1, 2, 3):
            ta = ta + r1a[(x + j) % 4, :, b * WB:(b + 1) * WB].astype(F32)
        a2[b] = ta
        for q in range(4):
            tb = acc[core, b, q * 128 + 64:q * 128 + 128, own_cols]
            for j in (1, 2, 3):
                tb = tb + r1b[(y + j) % 4, q, :, b * 128:b * 128 + 128].astype(F32)
            b2[b, q] = tb
            s2a[q, 64 * b:64 * b + 64, :] = ta[:, q * 128:q * 128 + 128].astype(BF)
            s2b[q, 64 * b:64 * b + 64, :] = tb.astype(BF)
    to = oown[core, pl.ds(own_x, 128), :]
    for j in (1, 2, 3):
        got = r1a[(x + j) % 4, :, width:width + 256].astype(F32)
        to = to + jnp.concatenate([got[:, 0:128], got[:, 128:256]], axis=0)
    for q in range(4):
        part = jnp.concatenate([to[zl * 32 + q * 8:zl * 32 + q * 8 + 8, :] for zl in range(4)], axis=0)
        oown[core, q * 32:q * 32 + 32, :] = part
        s2a[q, 128:160, :] = part.astype(BF)
    second = []
    for j in (1, 2, 3):
        xx, yy = (x + j) % 4, (y + j) % 4
        copy = remote(s2a.at[yy], r2a.at[y], a2sem, j, dev(x, yy, z, core))
        copy.start()
        second.append(copy)
        copy = remote(s2b.at[xx], r2b.at[x], b2sem, j, dev(xx, y, z, core))
        copy.start()
        second.append(copy)
    lax.fori_loop(per, 2 * per, hidden_step, 0)
    for copy in second:
        copy.wait_recv()

    empty = jnp.zeros((8, 128), F32)
    to = oown[core, pl.ds(pl.multiple_of(y * 32, 32), 32), :]
    for j in (1, 2, 3):
        to = to + r2a[(y + j) % 4, 128:160, :].astype(F32)
    sums = []
    for b in range(NWB):
        ta = a2[b, :, own_cols]
        tb = b2[b, x]
        for j in (1, 2, 3):
            ta = ta + r2a[(y + j) % 4, 64 * b:64 * b + 64, :].astype(F32)
            tb = tb + r2b[(x + j) % 4, 64 * b:64 * b + 64, :].astype(F32)
        sums.append((ta[0:32], ta[32:64], tb[0:32], tb[32:64]))
    for q in range(4):
        part = jnp.concatenate([sums[0][q], sums[1][q], to[q * 8:q * 8 + 8, :], empty], axis=0)
        z4[q] = part
        s3[q] = part.astype(BF)
    third = []
    for j in (4, 3, 5, 2, 6, 1, 7):
        zz = (z + j) % 8
        copy = remote(s3.at[zz % 4], r3.at[z], z3sem, j, dev(x, y, zz, core))
        copy.start()
        third.append(copy)
    total = z4[z_lo]
    for copy in third:
        copy.wait_recv()
    for j in range(1, 8):
        total = total + r3[(z + j) % 8].astype(F32)
    total = total * scale
    s4[...] = total.astype(BF)

    fourth = []
    for j in (1, 2, 3):
        copy = remote(s4, r4.at[y], y4sem, j, dev(x, (y + j) % 4, z, core))
        copy.start()
        fourth.append(copy)
    r4[y] = s4[...]
    for chunk in pred_copies + grad_copies:
        for copy in chunk:
            copy.wait_send()
    for copy in core_copies + first + second + third:
        copy.wait_send()
    for copy in fourth:
        copy.wait_recv()
    for q in range(4):
        got = r4[q].astype(F32)
        for b in range(NWB):
            win_out[:, b * WB + q * 128:b * WB + q * 128 + 128] = got[32 * b:32 * b + 32, :]
        wout_out[q * 8:q * 8 + 8, :] = got[64:72, 0:V]
    for copy in fourth:
        copy.wait_send()


def place(hg_in, in_in, out_in, hg_out, in_out, out_out, sem):
    points = hg_in.shape[1]
    parts = 8
    copies = []
    for i in range(parts):
        rows = pl.ds(i * (points // parts), points // parts)
        copies.append(pltpu.make_async_copy(hg_in.at[0, rows], hg_out.at[0, rows], sem.at[i]))
    copies.append(pltpu.make_async_copy(in_in, in_out, sem.at[parts]))
    copies.append(pltpu.make_async_copy(out_in, out_out, sem.at[parts + 1]))
    for copy in copies:
        copy.start()
    for copy in copies:
        copy.wait()


def shards(hidden, pred, target, area, var_weight, w_in, w_out):
    points, width = hidden.shape[1:]
    scale = 1.0 / math.sqrt(points * lax.axis_size("grid") * MEMBERS)
    share = width // lax.axis_size("grid")
    any_spec = pl.BlockSpec(memory_space=pl.ANY)
    vmem_spec = pl.BlockSpec(memory_space=pltpu.VMEM)

    def vm(*shape, dtype=BF):
        return pltpu.VMEM(shape, dtype)

    def sems(*shape):
        return pltpu.SemaphoreType.DMA(shape)

    out_types = (
        jax.ShapeDtypeStruct(hidden.shape, BF),
        jax.ShapeDtypeStruct((share, width), F32),
        jax.ShapeDtypeStruct((share, V), F32),
    )
    half = width // 2
    pb = points // (NCH * MEMBERS)
    results = pl.pallas_call(
        functools.partial(kernel, scale),
        out_shape=tuple(pltpu.VMEM(t.shape, t.dtype) for t in out_types),
        in_specs=[any_spec] * 7,
        out_specs=(vmem_spec, vmem_spec, vmem_spec),
        scratch_shapes=[
            vm(1, points, dtype=F32), vm(1, V, dtype=F32), vm(V, width),
            vm(points, width), vm(width, width), vm(2, half, points), vm(points, width),
            vm(points, width, dtype=F32), vm(points, width), vm(VP, width),
            vm(NCH, MEMBERS, V, pb), vm(NCH, MEMBERS, V, pb), vm(NCH, V, pb), vm(NCH, MEMBERS, VS, pb),
            vm(NCH * MEMBERS, VP, pb),
            vm(2, NWB, half, WB, dtype=F32), vm(NWB, half, WB), vm(NWB, half, WB),
            vm(VP, width, dtype=F32), vm(half, VP), vm(half, VP), vm(2, half, VP, dtype=F32),
            vm(4, 64, width + 256), vm(4, 4, 64, 256), vm(4, 64, width + 256), vm(4, 4, 64, 256),
            vm(NWB, 64, WB, dtype=F32), vm(NWB, 4, 64, 128, dtype=F32),
            vm(4, 160, 128), vm(4, 128, 128), vm(4, 160, 128), vm(4, 128, 128),
            vm(4, 80, 128, dtype=F32), vm(4, 80, 128), vm(8, 80, 128), vm(80, 128), vm(4, 80, 128),
            sems(3 + MEMBERS, 4), sems(points // BLK),
            sems(NCH, 2, MEMBERS), sems(NCH, 2, MEMBERS), sems(2, NWB + 1),
            sems(2, 4), sems(2, 4), sems(2, 4), sems(2, 4), sems(2, 8), sems(2, 4),
        ],
        compiler_params=pltpu.CompilerParams(
            collective_id=0, has_side_effects=True, vmem_limit_bytes=50 * 1024 * 1024
        ),
    )(hidden, pred, target, area.reshape(1, -1), var_weight.reshape(1, -1), w_in, w_out.T)
    return pl.pallas_call(
        place,
        out_shape=out_types,
        in_specs=[vmem_spec] * 3,
        out_specs=(any_spec,) * 3,
        scratch_shapes=[sems(10)],
        compiler_params=pltpu.CompilerParams(vmem_limit_bytes=8 * 1024 * 1024),
    )(*results)


def solution(mesh):
    return jax.shard_map(
        shards,
        mesh=mesh,
        in_specs=(
            P("member", "grid", None),
            P("member", None, "grid"),
            P(None, "grid"),
            P("grid"),
            P(),
            P(),
            P(),
        ),
        out_specs=(P("member", "grid", None), P("grid", None), P("grid", None)),
        check_vma=False,
    )
```
